256 devices in a mesh: dp: 16 (over z, x_lo), tensor: 16 (over x_hi, y, core).
Axes of the slice: x: 4 (x_hi: 2, x_lo: 2; x = x_hi * 2 + x_lo), y: 4, z: 8, core: 2. Of those that a mesh axis runs over, the one named last changes fastest.
Arguments:
- inputs: bfloat16 [3072, 4096], P('dp'), may hold values from -6 to 6
- gate_pre: bfloat16 [3072, 14784], P('dp', 'tensor'), may hold values from -6 to 6
- up_pre: bfloat16 [3072, 14784], P('dp', 'tensor'), may hold values from -6 to 6
- grad_hidden: bfloat16 [3072, 14784], P('dp', 'tensor'), may hold values from -6 to 6
- gate_up_weight: bfloat16 [2, 4096, 14784], P(None, 'dp', 'tensor'), may hold values from -0.046875 to 0.046875
- moment_code: bfloat16 [2, 4096, 14784], P(None, 'dp', 'tensor'), may hold values from -1 to 1
- second_code: bfloat16 [2, 4096, 14784], P(None, 'dp', 'tensor'), may hold values from 0.049804688 to 1
- moment_scale: float32 [2, 16, 14784], P(None, 'dp', 'tensor'), may hold values from 0.0005 to 0.005
- second_scale: float32 [2, 16, 14784], P(None, 'dp', 'tensor'), may hold values from 2e-06 to 2e-05
Outputs:
- input_grad: bfloat16 [3072, 4096], P('dp', 'tensor')
- adam_step: float32 [2, 4096, 14784], P(None, 'dp', 'tensor')
- moment_code_new: bfloat16 [2, 4096, 14784], P(None, 'dp', 'tensor')
- second_code_new: bfloat16 [2, 4096, 14784], P(None, 'dp', 'tensor')
- moment_scale_new: float32 [2, 16, 14784], P(None, 'dp', 'tensor')
- second_scale_new: float32 [2, 16, 14784], P(None, 'dp', 'tensor')
The draws below stay inside these ranges and needn't reach their ends.
All inputs are finite; a program needn't handle non-finite values. Where the reference program divides by a largest or mean magnitude, that divisor is 1e-20 or more.
Results may differ from the reference program's by a relative error of at most 0.025.
Values may be sent and summed in bfloat16 or wider, within the bound.
A program may use at most 128 MiB of HBM per device.

```python
import math
import jax
import jax.numpy as jnp
from jax import lax

DW = 4096
FF = 14784
BLOCK = 256
TOK_DEV = 192
TOKENS = 3072


def with_spikes(entries, key, source, target, shards_of, factor):
    owner, partner = [(jnp.arange(entries.shape[dim]) // (entries.shape[dim] // shards_of)).reshape([-1 if axis == dim else 1 for axis in range(entries.ndim)]) for dim in (source, target)]
    chosen = jax.random.permutation(key, shards_of)[partner]
    strong = (owner == chosen) | (owner == (partner + shards_of // 2) % shards_of)
    return jnp.where(strong, factor * entries, entries)


def level_of(own_key, shape, cuts, least, top_value):
    def one(position, blocks):
        draws = jax.random.uniform(jax.random.fold_in(jax.random.fold_in(own_key, 6), position), (blocks,), jnp.float32, least / len(cuts), top_value / len(cuts))
        return jnp.repeat(jnp.exp(draws), shape[position] // blocks).reshape((-1,) + (1,) * (len(shape) - position - 1))

    gain = one(*cuts[0])
    for cut in cuts[1:]:
        gain = gain * one(*cut)
    return gain


def bell_draw(rng, dims, scale, most, cuts=(), dtype=jnp.bfloat16):
    level = level_of(rng, dims, cuts, -0.22, 0.18) if cuts else 1.0
    values = jax.random.normal(rng, dims, jnp.float32) * scale * level
    return jnp.minimum(jnp.maximum(values, -most), most).astype(dtype)


def bell_draw_with(rng, extent, scale, reach, pieces, heavy, held_as=jnp.bfloat16):
    result = scale * jax.random.normal(rng, extent, jnp.float32)
    if pieces:
        result = result * level_of(rng, extent, pieces, -0.22, 0.18)
    return jnp.clip(with_spikes(result, jax.random.fold_in(rng, 3), *heavy), -reach, reach).astype(held_as)


def setup_inputs(seed: int = 0) -> dict:
    key_list = jax.random.split(jax.random.key(seed), 10)
    return {
        "inputs": bell_draw_with(key_list[0], (TOKENS, DW), 1.0, 6.0, ((0, 16),), (0, 1, 16, 2.0)),
        "gate_pre": bell_draw(key_list[1], (TOKENS, FF), 1.5, 6.0, ((0, 16), (1, 16))),
        "up_pre": bell_draw(key_list[2], (TOKENS, FF), 1.0, 6.0, ((0, 16), (1, 16))),
        "grad_hidden": bell_draw(key_list[3], (TOKENS, FF), 1.0, 6.0, ((0, 16), (1, 16))),
        "gate_up_weight": bell_draw(key_list[4], (2, DW, FF), FF ** -0.5, 0.046875, ((1, 16), (2, 16))),
        "moment_code": jnp.clip(jax.random.uniform(key_list[5], (2, DW, FF), jnp.float32, -1.0, 1.0) * level_of(key_list[5], (2, DW, FF), ((1, 16), (2, 16)), -0.4, 0.0), -1.0, 1.0).astype(jnp.bfloat16),
        "second_code": jnp.clip(0.049804688 + 0.9501953 * jax.random.uniform(key_list[6], (2, DW, FF), jnp.float32) ** level_of(key_list[6], (2, DW, FF), ((1, 16), (2, 16)), -0.2, 0.2), 0.049804688, 1.0).astype(jnp.bfloat16),
        "moment_scale": jnp.clip(jnp.exp(math.log(0.005) - 2.30258502 * jax.random.uniform(key_list[7], (2, DW // BLOCK, FF), jnp.float32) ** level_of(key_list[7], (2, DW // BLOCK, FF), ((1, 16), (2, 16)), -0.2, 0.2)), 0.0005, 0.005),
        "second_scale": jnp.clip(jnp.exp(math.log(1.9999999494757503e-05) - 2.3025851 * jax.random.uniform(key_list[8], (2, DW // BLOCK, FF), jnp.float32) ** level_of(key_list[8], (2, DW // BLOCK, FF), ((1, 16), (2, 16)), -0.2, 0.2)), 1.9999999949504854e-06, 1.9999999494757503e-05),
    }


beta_first = 0.9
beta_second = 0.95
bias_first = 0.19
bias_second = 0.0975
adam_eps = 1e-08
scale_eps = 1e-06

def silu_grads(gate_pre, up_pre, grad_hidden):
    gate = gate_pre.astype(jnp.float32)
    upper = up_pre.astype(jnp.float32)
    incoming = grad_hidden.astype(jnp.float32)
    sigmoid_gate = jax.nn.sigmoid(gate)
    grad_up = (incoming * gate * sigmoid_gate).astype(jnp.bfloat16)
    grad_gate = (incoming * upper * sigmoid_gate * (1.0 + gate * (1.0 - sigmoid_gate))).astype(jnp.bfloat16)
    return (grad_gate, grad_up)

def dequantize(block_code, block_scale):
    row_count, width = block_code.shape
    blocks = block_code.astype(jnp.float32).reshape(-1, BLOCK, width)
    return (blocks * block_scale[:, None, :]).reshape(row_count, width)

def requantize(values):
    row_count, width = values.shape
    blocks = values.reshape(-1, BLOCK, width)
    block_scale = lax.optimization_barrier(jnp.max(jnp.abs(blocks), axis=1)) + scale_eps
    block_code = (blocks / block_scale[:, None, :]).reshape(row_count, width).astype(jnp.bfloat16)
    return (block_code, block_scale)

def adam_update(weight_grad, moment_code, second_code, moment_scale, second_scale):
    moment = beta_first * dequantize(moment_code, moment_scale) + (1.0 - beta_first) * weight_grad
    second = beta_second * dequantize(second_code, second_scale) + (1.0 - beta_second) * weight_grad * weight_grad
    adam_step = moment / bias_first / (jnp.sqrt(second / bias_second) + adam_eps)
    moment_code_new, moment_scale_new = requantize(moment)
    second_code_new, second_scale_new = requantize(second)
    return (adam_step, moment_code_new, second_code_new, moment_scale_new, second_scale_new)

def reference(inputs, gate_pre, up_pre, grad_hidden, gate_up_weight, moment_code, second_code, moment_scale, second_scale):
    grad_gate, grad_up = silu_grads(gate_pre, up_pre, grad_hidden)
    input_grad = jnp.dot(grad_gate, gate_up_weight[0].T, preferred_element_type=jnp.float32)
    input_grad = (input_grad + jnp.dot(grad_up, gate_up_weight[1].T, preferred_element_type=jnp.float32)).astype(jnp.bfloat16)
    paired = jnp.concatenate([grad_gate, grad_up], axis=1)
    input_blocks = inputs.reshape(-1, TOK_DEV, DW)
    paired_blocks = paired.reshape(-1, TOK_DEV, 2 * FF)

    def accumulate(running, item):
        partial_term = jnp.dot(item[0].T, item[1], preferred_element_type=jnp.float32)
        rounded = lax.optimization_barrier(partial_term.astype(jnp.bfloat16)).astype(jnp.float32)
        return (running + rounded, None)
    running, _ = lax.scan(accumulate, jnp.zeros((DW, 2 * FF), jnp.float32), (input_blocks, paired_blocks))
    running = running / TOKENS
    weight_grad = jnp.stack([running[:, :FF], running[:, FF:]])
    results = lax.map(lambda items: adam_update(*items), (weight_grad, moment_code, second_code, moment_scale, second_scale))
    return (input_grad, results[0], results[1], results[2], results[3], results[4])
```

```python
import functools

import jax
import jax.numpy as jnp
from jax import lax
from jax.experimental import pallas as pl
from jax.experimental.pallas import tpu as pltpu
from jax.sharding import PartitionSpec as P

MESH = pl.DeviceIdType.MESH
F32 = jnp.float32
BF16 = jnp.bfloat16

beta_first = 0.9
beta_second = 0.95
bias_first = 0.19
bias_second = 0.0975
adam_eps = 1e-08
scale_eps = 1e-06

TOK = 192
HALF = 96
ROWS = 256
HID = 924
PACK = 1920
NZ = 8
NM = 8
TOKENS = 3072
QR = 48
LANE = 128

GROUPS = ((0, 384, 0), (384, 384, 768), (768, 128, 1536))
TAIL_AT = 1792
TAIL_FROM = 896
TAIL = HID - TAIL_FROM
CHUNKS = ((0, 768), (768, 768), (1536, 384))
LAST = len(CHUNKS) - 1


def slot_of(rel):
    rel = rel % NZ
    if rel == 0:
        return 0
    if rel == 4:
        return 7
    return 2 * rel if rel < 4 else 2 * (NZ - rel) - 1


REL_OF = {slot_of(rel): rel for rel in range(NZ)}
ROUNDS = ((0, 3), (3, 5), (5, 7), (7, 8))


def pack_tail(first, second):
    rows = first.shape[0]
    blank = jnp.zeros((rows, 64 - TAIL), first.dtype)
    return jnp.concatenate([first, blank, second, blank], axis=1)


def comm_kernel(
    x_hbm, gate_hbm, up_hbm, gh_hbm, w_hbm,
    wg_hbm, out_hbm,
    gate_v, up_v, gh_v, w_v, gbuf, xbuf, xt, wbuf, wt,
    dw_send, dw_recv, dw_own, c_send, c_recv, keep, rs_src, rs_recv, f_src, f_buf,
    load_sem, ring_s, ring_r, x1_s, x1_r, x2_s, x2_r, x3_s, x3_r, w_s, w_r,
    dw_s, dw_r, core_s, core_r, rs_s, rs_r, fin_s, fin_r, out_sem,
):
    d = lax.axis_index("dp")
    t = lax.axis_index("tensor")
    z, xl = d // 2, d % 2
    m, c = t // 2, t % 2
    y, xh = m % 4, m // 4

    def at_z(r):
        return (((z + r) % NZ) * 2 + xl, t)

    def at_m(e):
        return (d, ((m + e) % NM) * 2 + c)

    sibling = (d, m * 2 + (1 - c))
    partner = (z * 2 + (1 - xl), t)

    loads = [
        pltpu.make_async_copy(gate_hbm, gate_v, load_sem.at[0]),
        pltpu.make_async_copy(up_hbm, up_v, load_sem.at[1]),
        pltpu.make_async_copy(gh_hbm, gh_v, load_sem.at[2]),
        pltpu.make_async_copy(w_hbm, w_v, load_sem.at[3]),
    ]
    for load in loads:
        load.start()

    barrier = pltpu.get_barrier_semaphore()
    for r in range(1, NZ):
        pl.semaphore_signal(barrier, inc=1, device_id=at_z(r), device_id_type=MESH)
    for e in range(1, NM):
        pl.semaphore_signal(barrier, inc=1, device_id=at_m(e), device_id_type=MESH)
    pl.semaphore_signal(barrier, inc=1, device_id=sibling, device_id_type=MESH)
    pl.semaphore_signal(barrier, inc=1, device_id=partner, device_id_type=MESH)
    for source in range(NM):
        pl.semaphore_signal(
            barrier, inc=1, device_id=(m * 2 + xl, source * 2 + c), device_id_type=MESH
        )
    pl.semaphore_wait(barrier, 2 * (NZ - 1) + 2 + NM)

    sends = []

    def remote(src, dst, send_sem, recv_sem, where):
        return pltpu.make_async_remote_copy(
            src_ref=src, dst_ref=dst, send_sem=send_sem, recv_sem=recv_sem,
            device_id=where, device_id_type=MESH,
        )

    def launch(copy):
        copy.start()
        sends.append(copy)
        return copy

    q_at = pl.multiple_of(y * QR, 16)
    ct_at = pl.multiple_of((c * 2 + xh) * LANE, LANE)

    def x_columns(r):
        return pl.ds(pl.multiple_of(((z + r) % NZ) * 512 + (c * 2 + xh) * LANE, LANE), LANE)

    x_first = []
    for r in range(1, NZ):
        x_first.append(launch(remote(
            x_hbm.at[pl.ds(q_at, QR), x_columns(r)],
            xbuf.at[slot_of(-r), pl.ds(q_at, QR), pl.ds(ct_at, LANE)],
            x1_s.at[r], x1_r.at[r], at_z(r),
        )))
    x_own = pltpu.make_async_copy(
        x_hbm.at[pl.ds(q_at, QR), x_columns(0)],
        xbuf.at[0, pl.ds(q_at, QR), pl.ds(ct_at, LANE)], x1_r.at[0],
    )
    x_own.start()

    ring = {}
    for k, (start, width) in enumerate(CHUNKS):
        for s in range(1, 5):
            for way in range(2):
                for h in range(2):
                    if s == 4 and way != h:
                        continue
                    sign = -1 if way == 0 else 1
                    src_slot, dst_slot = slot_of(sign * (s - 1)), slot_of(sign * s)
                    rows, columns = pl.ds(h * HALF, HALF), pl.ds(start, width)
                    ring[k, s, way, h] = remote(
                        gbuf.at[src_slot, rows, columns],
                        gbuf.at[dst_slot, rows, columns],
                        ring_s.at[k, s - 1, way, h], ring_r.at[k, s - 1, way, h],
                        at_z(1 if way == 0 else -1),
                    )

    def grads(first, width):
        g = gate_v[:, first:first + width].astype(F32)
        u = up_v[:, first:first + width].astype(F32)
        h = gh_v[:, first:first + width].astype(F32)
        sig = jax.nn.sigmoid(g)
        g_up = (h * g * sig).astype(BF16)
        g_gate = (h * u * sig * (1.0 + g * (1.0 - sig))).astype(BF16)
        return g_gate, g_up

    def fill(k):
        first, width, at = GROUPS[k]
        g_gate, g_up = grads(first, width)
        gbuf[0, :, at:at + width] = g_gate
        gbuf[0, :, at + width:at + 2 * width] = g_up
        if k == LAST:
            g_gate, g_up = grads(TAIL_FROM, TAIL)
            gbuf[0, :, TAIL_AT:TAIL_AT + LANE] = pack_tail(g_gate, g_up)

    def first_step(k):
        for h in range(2):
            for way in range(2):
                launch(ring[k, 1, way, h])

    for load in loads[:3]:
        load.wait()
    fill(0)
    first_step(0)

    loads[3].wait()
    for first, width, at in GROUPS:
        wbuf[0, :, at:at + width] = w_v[0, :, first:first + width]
        wbuf[0, :, at + width:at + 2 * width] = w_v[1, :, first:first + width]
    wbuf[0, :, TAIL_AT:TAIL_AT + LANE] = pack_tail(
        w_v[0, :, TAIL_FROM:HID], w_v[1, :, TAIL_FROM:HID]
    )
    w_copy = launch(remote(wbuf.at[0], wbuf.at[1], w_s, w_r, partner))

    fill(1)

    def x_second():
        x_own.wait()
        for copy in x_first:
            copy.wait_recv()
        piece = xbuf.at[:, pl.ds(q_at, QR), pl.ds(ct_at, LANE)]
        for e in range(1, NM):
            launch(remote(piece, piece, x2_s.at[e], x2_r.at[e], at_m(e)))

    def x_third():
        for e in range(1, NM):
            src_m = (m + NM - e) % NM
            there = xbuf.at[
                :,
                pl.ds(pl.multiple_of((src_m % 4) * QR, 16), QR),
                pl.ds(pl.multiple_of((c * 2 + src_m // 4) * LANE, LANE), LANE),
            ]
            remote(there, there, x2_s.at[e], x2_r.at[e], at_m(e)).wait_recv()
        mine = xbuf.at[:, :, pl.ds(pl.multiple_of(c * 256, 256), 256)]
        launch(remote(mine, mine, x3_s, x3_r, sibling))

    def x_turn():
        theirs = xbuf.at[:, :, pl.ds(pl.multiple_of((1 - c) * 256, 256), 256)]
        remote(theirs, theirs, x3_s, x3_r, sibling).wait_recv()
        for j in range(2):
            for i in range(4):
                block = xbuf[2 * i:2 * i + 2, :, j * 256:(j + 1) * 256].reshape(2 * TOK, 256)
                xt[j, :, i * 2 * TOK:(i + 1) * 2 * TOK] = block.T

    def w_turn():
        w_copy.wait_recv()
        for which in range(2):
            j = xl if which == 0 else 1 - xl
            for i in range(5):
                wt[j, i * 384:(i + 1) * 384, :] = wbuf[which, :, i * 384:(i + 1) * 384].T

    dw_copies = {}

    def dw_product(j, first, width):
        block = gbuf[:, :, first:first + width].reshape(NZ * TOK, width)
        return jnp.dot(xt[j], block, preferred_element_type=F32)

    def dw_out(k):
        start, width = CHUNKS[k]
        for first in range(start, start + width, 384):
            dw_send[:, first:first + 384] = dw_product(1 - xl, first, 384).astype(BF16)
        columns = pl.ds(start, width)
        dw_copies[k] = launch(remote(
            dw_send.at[:, columns], dw_recv.at[:, columns], dw_s.at[k], dw_r.at[k], partner
        ))

    def dw_keep(k):
        start, width = CHUNKS[k]
        for first in range(start, start + width, 384):
            dw_own[:, first:first + 384] = dw_product(xl, first, 384)

    wg_copies = []

    def dw_end(k):
        start, width = CHUNKS[k]
        dw_copies[k].wait_recv()
        for first in range(start, start + width, 384):
            columns = slice(first, first + 384)
            dw_own[:, columns] = (dw_own[:, columns] + dw_recv[:, columns].astype(F32)) / TOKENS
        columns = pl.ds(start, width)
        copy = pltpu.make_async_copy(dw_own.at[:, columns], wg_hbm.at[:, columns], out_sem.at[k])
        copy.start()
        wg_copies.append(copy)

    core_copies = {}
    rs_copies = {}

    def dx_product(n):
        lo, hi = ROUNDS[n]
        block = gbuf[lo:hi].reshape((hi - lo) * TOK, PACK)
        there = jnp.dot(block, wt[1 - c], preferred_element_type=F32).astype(BF16)
        c_send[lo:hi] = there.reshape(hi - lo, TOK, 256)
        core_copies[n] = launch(remote(
            c_send.at[lo:hi], c_recv.at[lo:hi], core_s.at[n], core_r.at[n], sibling
        ))
        keep[lo:hi] = jnp.dot(block, wt[c], preferred_element_type=F32).reshape(hi - lo, TOK, 256)

    def dx_scatter(n):
        lo, hi = ROUNDS[n]
        core_copies[n].wait_recv()
        rs_src[lo:hi] = (keep[lo:hi] + c_recv[lo:hi].astype(F32)).astype(BF16)
        for e in range(1, NM):
            to = (m + e) % NM
            rs_copies[n, e] = launch(remote(
                rs_src.at[
                    lo:hi,
                    pl.ds(pl.multiple_of((to % 4) * QR, 16), QR),
                    pl.ds(pl.multiple_of((to // 4) * LANE, LANE), LANE),
                ],
                rs_recv.at[e, lo:hi],
                rs_s.at[n, e], rs_r.at[n, e], at_m(e),
            ))

    x_at = pl.multiple_of(xh * LANE, LANE)
    home = z == m
    fin_copies = {}

    def dx_finish(n):
        lo, hi = ROUNDS[n]
        for e in range(1, NM):
            rs_copies[n, e].wait_recv()
        total = rs_src[lo:hi, pl.ds(q_at, QR), pl.ds(x_at, LANE)].astype(F32)
        for e in range(1, NM):
            total = total + rs_recv[e, lo:hi].astype(F32)
        f_src[lo:hi] = total.astype(BF16)
        for p in range(lo, hi):
            rel = REL_OF[p]
            there = f_buf.at[pl.ds(q_at, QR), pl.ds(x_at, LANE)]
            copy = remote(
                f_src.at[p], there, fin_s.at[p], fin_r,
                (((z + rel) % NZ) * 2 + xl, z * 2 + c),
            )
            if rel:
                launch(copy)
            else:
                local = pltpu.make_async_copy(f_src.at[p], there, fin_r)
                pl.when(home)(local.start)
                pl.when(jnp.logical_not(home))(copy.start)
                fin_copies[0] = copy

    def after(k, s):
        if k == 0:
            if s == 1:
                x_second()
                fill(LAST)
            elif s == 2:
                x_third()
            elif s == 3:
                x_turn()
        elif k == 1:
            if s == 1:
                dw_out(0)
            elif s == 2:
                dw_keep(0)
            elif s == 3:
                w_turn()
            else:
                dw_end(0)
        else:
            if s == 1:
                dw_out(1)
                dx_product(0)
            elif s == 2:
                dx_scatter(0)
                dw_keep(1)
                dx_product(1)
            elif s == 3:
                dx_scatter(1)
                dx_finish(0)
                dx_product(2)
            else:
                dx_product(3)
                dw_out(2)
                dx_scatter(2)
                dx_scatter(3)
                dw_keep(2)
                dw_end(1)
                dx_finish(1)
                dx_finish(2)
                dx_finish(3)
                dw_end(2)

    for k in range(len(CHUNKS)):
        for s in range(1, 5):
            for h in range(2):
                for way in range(2):
                    if (k, s, way, h) not in ring:
                        continue
                    ring[k, s, way, h].wait_recv()
                    if (k, s + 1, way, h) in ring:
                        launch(ring[k, s + 1, way, h])
            if s == 3 and k < LAST:
                first_step(k + 1)
            after(k, s)

    pltpu.make_async_copy(f_buf, f_buf, fin_r).wait()
    result = pltpu.make_async_copy(f_buf, out_hbm, out_sem.at[LAST + 1])
    result.start()
    for copy in sends:
        copy.wait_send()
    pl.when(jnp.logical_not(home))(fin_copies[0].wait_send)
    for copy in wg_copies:
        copy.wait()
    result.wait()


def communicate(x, gate, up, gh, w):
    any_spec = pl.BlockSpec(memory_space=pl.ANY)
    dma = pltpu.SemaphoreType.DMA
    n = len(CHUNKS)
    return pl.pallas_call(
        comm_kernel,
        out_shape=(
            jax.ShapeDtypeStruct((ROWS, PACK), F32),
            jax.ShapeDtypeStruct((TOK, 256), BF16),
        ),
        in_specs=[any_spec] * 5,
        out_specs=(any_spec, any_spec),
        scratch_shapes=[
            pltpu.VMEM((TOK, HID), BF16),
            pltpu.VMEM((TOK, HID), BF16),
            pltpu.VMEM((TOK, HID), BF16),
            pltpu.VMEM((2, ROWS, HID), BF16),
            pltpu.VMEM((NZ, TOK, PACK), BF16),
            pltpu.VMEM((NZ, TOK, 512), BF16),
            pltpu.VMEM((2, 256, NZ * TOK), BF16),
            pltpu.VMEM((2, ROWS, PACK), BF16),
            pltpu.VMEM((2, PACK, 256), BF16),
            pltpu.VMEM((ROWS, PACK), BF16),
            pltpu.VMEM((ROWS, PACK), BF16),
            pltpu.VMEM((ROWS, PACK), F32),
            pltpu.VMEM((NZ, TOK, 256), BF16),
            pltpu.VMEM((NZ, TOK, 256), BF16),
            pltpu.VMEM((NZ, TOK, 256), F32),
            pltpu.VMEM((NZ, TOK, 256), BF16),
            pltpu.VMEM((NM, NZ, QR, LANE), BF16),
            pltpu.VMEM((NZ, QR, LANE), BF16),
            pltpu.VMEM((TOK, 256), BF16),
            dma((4,)),
            dma((n, 4, 2, 2)), dma((n, 4, 2, 2)),
            dma((NZ,)), dma((NZ,)),
            dma((NM,)), dma((NM,)),
            dma, dma, dma, dma,
            dma((n,)), dma((n,)),
            dma((4,)), dma((4,)),
            dma((4, NM)), dma((4, NM)),
            dma((NZ,)), dma,
            dma((n + 1,)),
        ],
        compiler_params=pltpu.CompilerParams(
            collective_id=0, has_side_effects=True, vmem_limit_bytes=48 * 1024 * 1024
        ),
        cost_estimate=pl.CostEstimate(
            flops=6_000_000_000, bytes_accessed=8_000_000, transcendentals=200_000
        ),
    )(x, gate, up, gh, w)


def adam_kernel(wg, mc, sc, ms, ss, step, mc_new, sc_new, ms_new, ss_new):
    p = pl.program_id(0)

    def piece(first, width, grad):
        columns = slice(first, first + width)
        moment = beta_first * (mc[0, :, columns].astype(F32) * ms[0, :, columns])
        moment = moment + (1.0 - beta_first) * grad
        second = beta_second * (sc[0, :, columns].astype(F32) * ss[0, :, columns])
        second = second + (1.0 - beta_second) * grad * grad
        step[0, :, columns] = moment / bias_first / (jnp.sqrt(second / bias_second) + adam_eps)
        m_scale = jnp.max(jnp.abs(moment), axis=0, keepdims=True) + scale_eps
        s_scale = jnp.max(jnp.abs(second), axis=0, keepdims=True) + scale_eps
        ms_new[0, :, columns] = m_scale
        ss_new[0, :, columns] = s_scale
        mc_new[0, :, columns] = (moment / m_scale).astype(BF16)
        sc_new[0, :, columns] = (second / s_scale).astype(BF16)

    for first, width, at in GROUPS:
        for inner in range(0, width, LANE):
            begin = pl.multiple_of(at + inner + p * width, LANE)
            piece(first + inner, LANE, wg[:, pl.ds(begin, LANE)])
    tail = wg[:, TAIL_AT:TAIL_AT + LANE]
    tail = jnp.where(p == 0, tail, pltpu.roll(tail, 64, 1))
    piece(TAIL_FROM, TAIL, tail[:, :TAIL])


def adam(wg, mc, sc, ms, ss):
    big = pl.BlockSpec((1, ROWS, HID), lambda p: (p, 0, 0))
    small = pl.BlockSpec((1, 1, HID), lambda p: (p, 0, 0))
    return pl.pallas_call(
        adam_kernel,
        grid=(2,),
        out_shape=(
            jax.ShapeDtypeStruct((2, ROWS, HID), F32),
            jax.ShapeDtypeStruct((2, ROWS, HID), BF16),
            jax.ShapeDtypeStruct((2, ROWS, HID), BF16),
            jax.ShapeDtypeStruct((2, 1, HID), F32),
            jax.ShapeDtypeStruct((2, 1, HID), F32),
        ),
        in_specs=[pl.BlockSpec((ROWS, PACK), lambda p: (0, 0)), big, big, small, small],
        out_specs=(big, big, big, small, small),
        compiler_params=pltpu.CompilerParams(vmem_limit_bytes=32 * 1024 * 1024),
    )(wg, mc, sc, ms, ss)


def per_device(x, gate, up, gh, w, mc, sc, ms, ss):
    wg, input_grad = communicate(x, gate, up, gh, w)
    return (input_grad,) + tuple(adam(wg, mc, sc, ms, ss))


def solution(mesh):
    whole = P(None, "dp", "tensor")
    token = P("dp", "tensor")
    return jax.shard_map(
        per_device,
        mesh=mesh,
        in_specs=(P("dp", None), token, token, token, whole, whole, whole, whole, whole),
        out_specs=(token, whole, whole, whole, whole, whole),
        check_vma=False,
    )
```

```python
import functools

import jax
import jax.numpy as jnp
from jax import lax
from jax.experimental import pallas as pl
from jax.experimental.pallas import tpu as pltpu
from jax.sharding import PartitionSpec as P

MESH = pl.DeviceIdType.MESH
F32 = jnp.float32
BF16 = jnp.bfloat16

beta_first = 0.9
beta_second = 0.95
bias_first = 0.19
bias_second = 0.0975
adam_eps = 1e-08
scale_eps = 1e-06

TOK = 192
HALF = 96
ROWS = 256
HID = 924
PACK = 1920
NZ = 8
NM = 8
NY = 4
TOKENS = 3072
QR = 48
LANE = 128

GROUPS = ((0, 384, 0), (384, 384, 768), (768, 128, 1536))
TAIL_AT = 1792
TAIL_FROM = 896
TAIL = HID - TAIL_FROM
CHUNKS = tuple((start, 384) for start in range(0, PACK, 384))
A, B, C, D, E = range(5)
VIEW = 4 * HID
VIEW_PAD = 4 * 960


OUTS = (
    jax.ShapeDtypeStruct((TOK, 256), BF16),
    jax.ShapeDtypeStruct((VIEW, LANE), F32),
    jax.ShapeDtypeStruct((VIEW, LANE), BF16),
    jax.ShapeDtypeStruct((VIEW, LANE), BF16),
    jax.ShapeDtypeStruct((2, 1, HID), F32),
    jax.ShapeDtypeStruct((2, 1, HID), F32),
)


def slot_of(rel):
    rel = rel % NZ
    if rel == 0:
        return 0
    if rel == 4:
        return 7
    return 2 * rel if rel < 4 else 2 * (NZ - rel) - 1


REL_OF = {slot_of(rel): rel for rel in range(NZ)}
ROUNDS = ((0, 1), (1, 3), (3, 5), (5, 7), (7, 8))


def pack_tail(first, second):
    rows = first.shape[0]
    blank = jnp.zeros((rows, 64 - TAIL), first.dtype)
    return jnp.concatenate([first, blank, second, blank], axis=1)


def comm_kernel(
    x_hbm, gate_hbm, up_hbm, gh_hbm, w_hbm, mc_hbm, sc_hbm, ms_hbm, ss_hbm,
    ig_out, step_out, mc_out, sc_out, ms_out, ss_out,
    gate_v, up_v, gh_v, w_v, w_f, mc_v, sc_v, ms_v, ss_v, ms_n, ss_n, m_f, s_f, step_v,
    gbuf, xbuf, xt, wt, dw_send, dw_recv, dw_own, c_send, c_recv, keep, rs_src, rs_recv, f_src, f_here, f_buf, out_v,
    load_sem, ring_s, ring_r, x1_s, x1_r, x2_s, x2_r, x3_s, x3_r, w_s, w_r,
    dw_s, dw_r, core_s, core_r, rs_s, rs_r, fz_s, fz_r, fin_s, fin_r, out_sem,
):
    d = lax.axis_index("dp")
    t = lax.axis_index("tensor")
    z, xl = d // 2, d % 2
    m, c = t // 2, t % 2
    y, xh = m % 4, m // 4

    def at_z(r):
        return (((z + r) % NZ) * 2 + xl, t)

    def at_y(e):
        return (d, (xh * 4 + (y + e) % NY) * 2 + c)

    def at_m(chip):
        return (d, (chip % NM) * 2 + c)

    sibling = (d, m * 2 + (1 - c))
    partner = (z * 2 + (1 - xl), t)

    loads = [
        pltpu.make_async_copy(gate_hbm, gate_v, load_sem.at[0]),
        pltpu.make_async_copy(up_hbm, up_v, load_sem.at[1]),
        pltpu.make_async_copy(gh_hbm, gh_v, load_sem.at[2]),
        pltpu.make_async_copy(w_hbm, w_v, load_sem.at[3]),
        pltpu.make_async_copy(mc_hbm, mc_v, load_sem.at[4]),
        pltpu.make_async_copy(sc_hbm, sc_v, load_sem.at[5]),
        pltpu.make_async_copy(ms_hbm, ms_v, load_sem.at[6]),
        pltpu.make_async_copy(ss_hbm, ss_v, load_sem.at[7]),
    ]
    for load in loads[:3]:
        load.start()

    barrier = pltpu.get_barrier_semaphore()
    for r in range(1, NZ):
        pl.semaphore_signal(barrier, inc=1, device_id=at_z(r), device_id_type=MESH)
    for e in range(1, NM):
        pl.semaphore_signal(barrier, inc=1, device_id=at_m(m + e), device_id_type=MESH)
    pl.semaphore_signal(barrier, inc=1, device_id=sibling, device_id_type=MESH)
    pl.semaphore_signal(barrier, inc=1, device_id=partner, device_id_type=MESH)

    sends = []

    def remote(src, dst, send_sem, recv_sem, where):
        return pltpu.make_async_remote_copy(
            src_ref=src, dst_ref=dst, send_sem=send_sem, recv_sem=recv_sem,
            device_id=where, device_id_type=MESH,
        )

    def launch(copy):
        copy.start()
        sends.append(copy)
        return copy

    def grads(first, width):
        g = gate_v[:, first:first + width].astype(F32)
        u = up_v[:, first:first + width].astype(F32)
        h = gh_v[:, first:first + width].astype(F32)
        sig = jax.nn.sigmoid(g)
        g_up = (h * g * sig).astype(BF16)
        g_gate = (h * u * sig * (1.0 + g * (1.0 - sig))).astype(BF16)
        return g_gate, g_up

    def fill(k):
        first, width, at = GROUPS[k]
        g_gate, g_up = grads(first, width)
        gbuf[0, :, at:at + width] = g_gate
        gbuf[0, :, at + width:at + 2 * width] = g_up

    def fill_tail():
        g_gate, g_up = grads(TAIL_FROM, TAIL)
        gbuf[0, :, TAIL_AT:TAIL_AT + LANE] = pack_tail(g_gate, g_up)

    ring = {}
    for k, (start, width) in enumerate(CHUNKS):
        for s in range(1, 5):
            for way in range(2):
                for h in range(2):
                    if s == 4 and way != h:
                        continue
                    sign = -1 if way == 0 else 1
                    src_slot, dst_slot = slot_of(sign * (s - 1)), slot_of(sign * s)
                    rows, columns = pl.ds(h * HALF, HALF), pl.ds(start, width)
                    ring[k, s, way, h] = remote(
                        gbuf.at[src_slot, rows, columns],
                        gbuf.at[dst_slot, rows, columns],
                        ring_s.at[k, s - 1, way, h], ring_r.at[k, s - 1, way, h],
                        at_z(1 if way == 0 else -1),
                    )

    def step(k, s):
        for h in range(2):
            for way in range(2):
                if (k, s, way, h) in ring:
                    if s > 1:
                        ring[k, s - 1, way, h].wait_recv()
                    launch(ring[k, s, way, h])

    def third(k):
        for way in range(2):
            ring[k, 3, way, 1 - way].wait_recv()

    def fourth(k):
        for way in range(2):
            ring[k, 4, way, way].wait_recv()

    q_at = pl.multiple_of(y * QR, 16)
    core_half = pl.ds(pl.multiple_of(c * 256, 256), 256)

    def x_columns(r):
        return pl.ds(pl.multiple_of(((z + r) % NZ) * 512 + c * 256, 256), 256)

    x_first = []
    x_own = pltpu.make_async_copy(
        x_hbm.at[pl.ds(q_at, QR), x_columns(0)],
        xbuf.at[0, pl.ds(q_at, QR), core_half], x1_r.at[0],
    )

    def x_start():
        x_own.start()
        for r in range(1, NZ):
            x_first.append(launch(remote(
                x_hbm.at[pl.ds(q_at, QR), x_columns(r)],
                xbuf.at[slot_of(-r), pl.ds(q_at, QR), core_half],
                x1_s.at[r], x1_r.at[r], at_z(r),
            )))

    def x_second():
        x_own.wait()
        for copy in x_first:
            copy.wait_recv()
        piece = xbuf.at[:, pl.ds(q_at, QR), core_half]
        for e in range(1, NY):
            launch(remote(piece, piece, x2_s.at[e], x2_r.at[e], at_y(e)))

    def x_third():
        for e in range(1, NY):
            rows = pl.ds(pl.multiple_of(((y + NY - e) % NY) * QR, 16), QR)
            there = xbuf.at[:, rows, core_half]
            remote(there, there, x2_s.at[e], x2_r.at[e], at_y(e)).wait_recv()
        mine = xbuf.at[:, :, core_half]
        launch(remote(mine, mine, x3_s, x3_r, sibling))

    def x_turn():
        theirs = xbuf.at[:, :, pl.ds(pl.multiple_of((1 - c) * 256, 256), 256)]
        remote(theirs, theirs, x3_s, x3_r, sibling).wait_recv()
        for j in range(2):
            for i in range(4):
                block = xbuf[2 * i:2 * i + 2, :, j * 256:(j + 1) * 256].reshape(2 * TOK, 256)
                xt[j, :, i * 2 * TOK:(i + 1) * 2 * TOK] = block.T

    mine_w = wt.at[xl]
    w_copy = remote(mine_w, mine_w, w_s, w_r, partner)

    def w_prepare():
        loads[3].wait()
        w_f[:VIEW, :] = w_v[...].astype(F32)
        w_f[VIEW:, :] = jnp.zeros((VIEW_PAD - VIEW, LANE), F32)
        for p in range(2):
            for tile in range(2):
                lanes = slice(tile * LANE, (tile + 1) * LANE)
                for first, width, at in GROUPS + ((TAIL_FROM, 64, TAIL_AT),):
                    piece = w_f[pl.ds(first * 4 + tile * 2 + p, width, stride=4), :]
                    wt[xl, at + p * width:at + (p + 1) * width, lanes] = piece.astype(BF16)
        launch(w_copy)

    def w_wait():
        theirs = wt.at[1 - xl]
        remote(theirs, theirs, w_s, w_r, partner).wait_recv()

    dw_copies = {}

    def dw_product(j, k):
        start, width = CHUNKS[k]
        block = gbuf[:, :, start:start + width].reshape(NZ * TOK, width)
        return jnp.dot(xt[j], block, preferred_element_type=F32)

    def dw_out(k):
        start, width = CHUNKS[k]
        dw_send[:, start:start + width] = dw_product(1 - xl, k).astype(BF16)
        columns = pl.ds(start, width)
        dw_copies[k] = launch(remote(
            dw_send.at[:, columns], dw_recv.at[:, columns], dw_s.at[k], dw_r.at[k], partner
        ))

    def dw_keep(k):
        start, width = CHUNKS[k]
        dw_own[:, start:start + width] = dw_product(xl, k)

    out_copies = []

    def codes_prepare():
        for load in loads[4:]:
            load.wait()
        m_f[:VIEW, :] = mc_v[...].astype(F32)
        s_f[:VIEW, :] = sc_v[...].astype(F32)
        m_f[VIEW:, :] = jnp.zeros((VIEW_PAD - VIEW, LANE), F32)
        s_f[VIEW:, :] = jnp.zeros((VIEW_PAD - VIEW, LANE), F32)

    def column(ref, hidden, p):
        if hidden == TAIL_FROM:
            blank = jnp.ones((1, LANE - TAIL), F32)
            row = jnp.concatenate([ref[p, :, TAIL_FROM:HID], blank], axis=1)
        else:
            row = ref[p, :, hidden:hidden + LANE]
        return jnp.broadcast_to(row, (LANE, LANE)).T

    def top(parts):
        largest = jnp.maximum(jnp.abs(parts[0]), jnp.abs(parts[1]))
        largest = jnp.max(largest, axis=1, keepdims=True) + scale_eps
        return jnp.broadcast_to(largest, parts[0].shape)

    def adam(grads_by_tile, hidden, p):
        count = grads_by_tile[0].shape[0]
        m_scale = beta_first * column(ms_v, hidden, p)[:count]
        s_scale = beta_second * column(ss_v, hidden, p)[:count]
        places = [pl.ds(hidden * 4 + tile * 2 + p, count, stride=4) for tile in range(2)]
        moments, seconds = [], []
        for place, grad in zip(places, grads_by_tile):
            moment = m_f[place, :] * m_scale + (1.0 - beta_first) * grad
            second = s_f[place, :] * s_scale + (1.0 - beta_second) * grad * grad
            scale = jnp.sqrt(second * (1.0 / bias_second)) + adam_eps
            step_v[place, :] = moment * (1.0 / bias_first) / scale
            moments.append(moment)
            seconds.append(second)
        for values, store, new in ((moments, m_f, ms_n), (seconds, s_f, ss_n)):
            largest = top(values)
            if count < LANE:
                new[p, :, TAIL_FROM:HID] = largest.T[:1, :TAIL]
            else:
                new[p, :, hidden:hidden + LANE] = largest.T[:1]
            inverse = 1.0 / largest
            for place, value in zip(places, values):
                store[place, :] = value * inverse

    def dw_end(k):
        dw_copies[k].wait_recv()
        start, width = CHUNKS[k]
        for at in range(start, start + width, LANE):
            columns = slice(at, at + LANE)
            total = (dw_own[:, columns] + dw_recv[:, columns].astype(F32)) * (1.0 / TOKENS)
            total = total.T
            if at == TAIL_AT:
                places = ((0, 64, TAIL_FROM, 0), (64, 64, TAIL_FROM, 1))
            else:
                first, size, begin = [g for g in GROUPS if g[2] <= at][-1]
                p, inner = (at - begin) // size, (at - begin) % size
                places = ((0, LANE, first + inner, p),)
            for lo, count, hidden, p in places:
                adam([total[lo:lo + count, :LANE], total[lo:lo + count, LANE:]], hidden, p)

    def adam_out(i):
        lo, hi = ((0, 1536), (1536, 3072), (3072, VIEW))[i]
        mc_v[lo:hi, :] = m_f[lo:hi, :].astype(BF16)
        sc_v[lo:hi, :] = s_f[lo:hi, :].astype(BF16)
        rows = pl.ds(lo, hi - lo)
        pairs = [(step_v, step_out), (mc_v, mc_out), (sc_v, sc_out)]
        copies = [
            pltpu.make_async_copy(src.at[rows], dst.at[rows], out_sem.at[i, q])
            for q, (src, dst) in enumerate(pairs)
        ]
        if i == 2:
            copies.append(pltpu.make_async_copy(ms_n, ms_out, out_sem.at[i, 3]))
            copies.append(pltpu.make_async_copy(ss_n, ss_out, out_sem.at[i, 4]))
        for copy in copies:
            copy.start()
        out_copies.extend(copies)

    core_copies = {}
    rs_copies = {}

    def dx_away(n):
        lo, hi = ROUNDS[n]
        block = gbuf[lo:hi].reshape((hi - lo) * TOK, PACK)
        there = jnp.dot(block, wt[1 - c], preferred_element_type=F32).astype(BF16)
        c_send[lo:hi] = there.reshape(hi - lo, TOK, 256)
        core_copies[n] = launch(remote(
            c_send.at[lo:hi], c_recv.at[lo:hi], core_s.at[n], core_r.at[n], sibling
        ))

    def dx_keep(n):
        lo, hi = ROUNDS[n]
        block = gbuf[lo:hi].reshape((hi - lo) * TOK, PACK)
        keep[lo:hi] = jnp.dot(block, wt[c], preferred_element_type=F32).reshape(hi - lo, TOK, 256)

    def dx_scatter(n):
        lo, hi = ROUNDS[n]
        core_copies[n].wait_recv()
        rs_src[lo:hi] = (keep[lo:hi] + c_recv[lo:hi].astype(F32)).astype(BF16)
        for e in range(1, NY):
            to = pl.ds(pl.multiple_of(((y + e) % NY) * QR, 16), QR)
            rs_copies[n, e] = launch(remote(
                rs_src.at[lo:hi, to], rs_recv.at[e, lo:hi], rs_s.at[n, e], rs_r.at[n, e], at_y(e)
            ))

    def dx_finish(n):
        lo, hi = ROUNDS[n]
        for e in range(1, NY):
            rs_copies[n, e].wait_recv()
        total = rs_src[lo:hi, pl.ds(q_at, QR)].astype(F32)
        for e in range(1, NY):
            total = total + rs_recv[e, lo:hi].astype(F32)
        if lo == 0:
            f_here[0:1] = total.astype(BF16)
            return
        f_src[lo:hi] = total.astype(BF16)
        for p in range(lo, hi):
            q = slot_of(-REL_OF[p])
            launch(remote(f_src.at[p], f_here.at[q], fz_s.at[q], fz_r.at[q], at_z(REL_OF[p])))

    home_copies = []

    def dx_home(n):
        for p in range(*ROUNDS[n]):
            rel = REL_OF[p]
            if p:
                there = f_here.at[p]
                remote(there, there, fz_s.at[p], fz_r.at[p], at_z(1)).wait_recv()
            chip = (z + rel) % NM
            target = f_buf.at[xh, pl.ds(q_at, QR)]
            away = remote(f_here.at[p], target, fin_s.at[p], fin_r, at_m(chip))
            local = pltpu.make_async_copy(f_here.at[p], target, fin_r)
            here = chip == m
            pl.when(here)(local.start)
            pl.when(jnp.logical_not(here))(away.start)
            home_copies.append((here, away))

    for load in loads[:3]:
        load.wait()
    fill(0)
    pl.semaphore_wait(barrier, (NZ - 1) + (NM - 1) + 2)

    step(A, 1)
    x_start()
    step(B, 1)
    for load in loads[3:]:
        load.start()
    fill(1)
    fill(2)
    fill_tail()
    step(A, 2)
    w_prepare()
    step(B, 2)
    x_second()
    step(A, 3)
    step(C, 1)
    codes_prepare()
    step(A, 4)
    x_third()
    step(B, 3)
    x_turn()
    step(C, 2)
    third(A)
    fourth(A)
    dw_out(A)
    dw_keep(A)
    step(B, 4)
    step(D, 1)
    step(C, 3)
    third(B)
    fourth(B)
    dw_out(B)
    dw_keep(B)
    step(D, 2)
    dw_end(A)
    step(C, 4)
    w_wait()
    dx_away(0)
    step(E, 1)
    dx_keep(0)
    step(D, 3)
    third(C)
    fourth(C)
    dw_out(C)
    dw_keep(C)
    dx_scatter(0)
    step(E, 2)
    dx_away(1)
    dx_keep(1)
    step(D, 4)
    dx_scatter(1)
    dw_end(B)
    adam_out(0)
    dx_finish(0)
    step(E, 3)
    dx_home(0)
    dx_away(2)
    dx_keep(2)
    dx_scatter(2)
    dx_finish(1)
    third(D)
    fourth(D)
    dw_out(D)
    step(E, 4)
    dw_keep(D)
    third(E)
    dx_away(3)
    dx_keep(3)
    dx_scatter(3)
    fourth(E)
    dx_away(4)
    dw_out(E)
    dx_keep(4)
    dx_scatter(4)
    dx_finish(2)
    dw_keep(E)
    dx_home(1)
    dx_finish(3)
    dw_end(C)
    dx_finish(4)
    dx_home(2)
    dw_end(D)
    adam_out(1)
    dx_home(3)
    dx_home(4)
    dw_end(E)
    adam_out(2)

    pltpu.make_async_copy(f_buf, f_buf, fin_r).wait()
    out_v[...] = (f_buf[0].astype(F32) + f_buf[1].astype(F32)).astype(BF16)
    result = pltpu.make_async_copy(out_v, ig_out, out_sem.at[0, 3])
    result.start()
    for copy in sends:
        copy.wait_send()
    for here, away in home_copies:
        pl.when(jnp.logical_not(here))(away.wait_send)
    for copy in out_copies:
        copy.wait()
    result.wait()


def compute(*operands):
    hbm = pl.BlockSpec(memory_space=pltpu.HBM)
    dma = pltpu.SemaphoreType.DMA
    n = len(CHUNKS)
    return pl.pallas_call(
        comm_kernel,
        out_shape=OUTS,
        in_specs=[hbm] * 9,
        out_specs=[pl.BlockSpec(memory_space=pl.ANY)] * 6,
        scratch_shapes=[
            pltpu.VMEM((TOK, HID), BF16),
            pltpu.VMEM((TOK, HID), BF16),
            pltpu.VMEM((TOK, HID), BF16),
            pltpu.VMEM((VIEW, LANE), BF16),
            pltpu.VMEM((VIEW_PAD, LANE), F32),
            pltpu.VMEM((VIEW, LANE), BF16),
            pltpu.VMEM((VIEW, LANE), BF16),
            pltpu.VMEM((2, 1, HID), F32),
            pltpu.VMEM((2, 1, HID), F32),
            pltpu.VMEM((2, 1, HID), F32),
            pltpu.VMEM((2, 1, HID), F32),
            pltpu.VMEM((VIEW_PAD, LANE), F32),
            pltpu.VMEM((VIEW_PAD, LANE), F32),
            pltpu.VMEM((VIEW_PAD, LANE), F32),
            pltpu.VMEM((NZ, TOK, PACK), BF16),
            pltpu.VMEM((NZ, TOK, 512), BF16),
            pltpu.VMEM((2, 256, NZ * TOK), BF16),
            pltpu.VMEM((2, PACK, 256), BF16),
            pltpu.VMEM((ROWS, PACK), BF16),
            pltpu.VMEM((ROWS, PACK), BF16),
            pltpu.VMEM((ROWS, PACK), F32),
            pltpu.VMEM((NZ, TOK, 256), BF16),
            pltpu.VMEM((NZ, TOK, 256), BF16),
            pltpu.VMEM((NZ, TOK, 256), F32),
            pltpu.VMEM((NZ, TOK, 256), BF16),
            pltpu.VMEM((NY, NZ, QR, 256), BF16),
            pltpu.VMEM((NZ, QR, 256), BF16),
            pltpu.VMEM((NZ, QR, 256), BF16),
            pltpu.VMEM((2, TOK, 256), BF16),
            pltpu.VMEM((TOK, 256), BF16),
            dma((8,)),
            dma((n, 4, 2, 2)), dma((n, 4, 2, 2)),
            dma((NZ,)), dma((NZ,)),
            dma((NY,)), dma((NY,)),
            dma, dma, dma, dma,
            dma((n,)), dma((n,)),
            dma((5,)), dma((5,)),
            dma((5, NY)), dma((5, NY)),
            dma((NZ,)), dma((NZ,)),
            dma((NZ,)), dma,
            dma((3, 5)),
        ],
        compiler_params=pltpu.CompilerParams(
            collective_id=0, has_side_effects=True, vmem_limit_bytes=60 * 1024 * 1024
        ),
        cost_estimate=pl.CostEstimate(
            flops=6_000_000_000, bytes_accessed=12_000_000, transcendentals=700_000
        ),
    )(*operands)


PIECES = tuple(
    (which, lo, min(lo + 1232, VIEW)) for lo in range(0, VIEW, 1232) for which in (1, 2, 3)
) + ((0, 0, TOK), (4, 0, 2), (5, 0, 2))


def place_kernel(*refs):
    sources, results, held, sem = refs[:6], refs[6:12], refs[12:18], refs[18]

    def moves(n, first, second):
        which, lo, hi = PIECES[n]
        rows = pl.ds(lo, hi - lo)
        return pltpu.make_async_copy(first[which].at[rows], second[which].at[rows], sem.at[n])

    arrivals = [moves(n, sources, held) for n in range(len(PIECES))]
    for copy in arrivals:
        copy.start()
    departures = []
    for n, copy in enumerate(arrivals):
        copy.wait()
        departures.append(moves(n, held, results))
        departures[-1].start()
    for copy in departures:
        copy.wait()


def place(*results):
    hbm = pl.BlockSpec(memory_space=pltpu.HBM)
    return pl.pallas_call(
        place_kernel,
        out_shape=OUTS,
        in_specs=[hbm] * 6,
        out_specs=[hbm] * 6,
        scratch_shapes=[pltpu.VMEM(out.shape, out.dtype) for out in OUTS]
        + [pltpu.SemaphoreType.DMA((len(PIECES),))],
        compiler_params=pltpu.CompilerParams(vmem_limit_bytes=60 * 1024 * 1024),
    )(*results)


def view(a):
    a = a.transpose(2, 0, 1).reshape(HID, 2, 2, LANE)
    return a.transpose(0, 2, 1, 3).reshape(VIEW, LANE)


def unview(a):
    a = a.reshape(HID, 2, 2, LANE).transpose(0, 2, 1, 3)
    return a.reshape(HID, 2, ROWS).transpose(1, 2, 0)


def per_device(x, gate, up, gh, w, mc, sc, ms, ss):
    results = compute(x, gate, up, gh, view(w), view(mc), view(sc), ms, ss)
    ig, step, mc_new, sc_new, ms_new, ss_new = place(*results)
    return ig, unview(step), unview(mc_new), unview(sc_new), ms_new, ss_new


def solution(mesh):
    whole = P(None, "dp", "tensor")
    token = P("dp", "tensor")
    return jax.shard_map(
        per_device,
        mesh=mesh,
        in_specs=(P("dp", None), token, token, token, whole, whole, whole, whole, whole),
        out_specs=(token, whole, whole, whole, whole, whole),
        check_vma=False,
    )
```

```python
import functools

import jax
import jax.numpy as jnp
from jax import lax
from jax.experimental import pallas as pl
from jax.experimental.pallas import tpu as pltpu
from jax.sharding import PartitionSpec as P

MESH = pl.DeviceIdType.MESH
F32 = jnp.float32
BF16 = jnp.bfloat16

beta_first = 0.9
beta_second = 0.95
bias_first = 0.19
bias_second = 0.0975
adam_eps = 1e-08
scale_eps = 1e-06

TOK = 192
HALF = 96
ROWS = 256
HID = 924
PACK = 1920
NZ = 8
NM = 8
NY = 4
TOKENS = 3072
QR = 48
LANE = 128

GROUPS = ((0, 384, 0), (384, 384, 768), (768, 128, 1536))
TAIL_AT = 1792
TAIL_FROM = 896
TAIL = HID - TAIL_FROM
FOLD = 640
CHUNKS = tuple((start, 384) for start in range(0, PACK, 384))
A, B, C, D, E = range(5)
VIEW = 4 * HID
VIEW_PAD = 4 * 960


OUTS = (
    jax.ShapeDtypeStruct((TOK, 256), BF16),
    jax.ShapeDtypeStruct((VIEW, LANE), F32),
    jax.ShapeDtypeStruct((VIEW, LANE), BF16),
    jax.ShapeDtypeStruct((VIEW, LANE), BF16),
    jax.ShapeDtypeStruct((2, 1, HID), F32),
    jax.ShapeDtypeStruct((2, 1, HID), F32),
)


def slot_of(rel):
    rel = rel % NZ
    if rel == 0:
        return 0
    if rel == 4:
        return 7
    return 2 * rel if rel < 4 else 2 * (NZ - rel) - 1


REL_OF = {slot_of(rel): rel for rel in range(NZ)}
ROUNDS = ((0, 1), (1, 3), (3, 5), (5, 7), (7, 8))


def pack_tail(first, second):
    rows = first.shape[0]
    blank = jnp.zeros((rows, 64 - TAIL), first.dtype)
    return jnp.concatenate([first, blank, second, blank], axis=1)


def comm_kernel(
    x_hbm, gate_hbm, up_hbm, gh_hbm, w_hbm, mc_hbm, sc_hbm, ms_hbm, ss_hbm,
    ig_out, step_out, mc_out, sc_out, ms_out, ss_out,
    gate_v, up_v, gh_v, w_v, w_f, mc_v, sc_v, ms_v, ss_v, ms_n, ss_n, m_f, s_f, step_v,
    gbuf, fold, xbuf, xt, wt, dw_send, dw_recv, dw_own, c_send, c_recv, keep, rs_src, rs_recv, f_src, f_here, f_buf, out_v,
    load_sem, ring_s, ring_r, x1_s, x1_r, x2_s, x2_r, x3_s, x3_r, w_s, w_r,
    dw_s, dw_r, core_s, core_r, rs_s, rs_r, fz_s, fz_r, fin_s, fin_r, out_sem,
    z_near, z_far, y_near, plane_in,
):
    d = lax.axis_index("dp")
    t = lax.axis_index("tensor")
    z, xl = d // 2, d % 2
    m, c = t // 2, t % 2
    y, xh = m % 4, m // 4

    def at_z(r):
        return (((z + r + NZ) % NZ) * 2 + xl, t)

    def at_y(e):
        return (d, (xh * 4 + (y + e + NY) % NY) * 2 + c)

    def at_m(chip):
        return (d, (chip % NM) * 2 + c)

    sibling = (d, m * 2 + (1 - c))
    partner = (z * 2 + (1 - xl), t)

    loads = [
        pltpu.make_async_copy(gate_hbm, gate_v, load_sem.at[0]),
        pltpu.make_async_copy(up_hbm, up_v, load_sem.at[1]),
        pltpu.make_async_copy(gh_hbm, gh_v, load_sem.at[2]),
        pltpu.make_async_copy(w_hbm, w_v, load_sem.at[3]),
        pltpu.make_async_copy(mc_hbm, mc_v, load_sem.at[4]),
        pltpu.make_async_copy(sc_hbm, sc_v, load_sem.at[5]),
        pltpu.make_async_copy(ms_hbm, ms_v, load_sem.at[6]),
        pltpu.make_async_copy(ss_hbm, ss_v, load_sem.at[7]),
    ]
    for load in loads[:3]:
        load.start()

    def tell(sem, devices):
        for device in devices:
            pl.semaphore_signal(sem, inc=1, device_id=device, device_id_type=MESH)

    barrier = pltpu.get_barrier_semaphore()
    near = [at_z(1), at_z(-1), at_y(1), at_y(-1), at_m(m + 4), sibling, partner]
    tell(barrier, near)

    sends = []

    def remote(src, dst, send_sem, recv_sem, where):
        return pltpu.make_async_remote_copy(
            src_ref=src, dst_ref=dst, send_sem=send_sem, recv_sem=recv_sem,
            device_id=where, device_id_type=MESH,
        )

    def launch(copy):
        copy.start()
        sends.append(copy)
        return copy

    def grads(first, width):
        g = gate_v[:, first:first + width].astype(F32)
        u = up_v[:, first:first + width].astype(F32)
        h = gh_v[:, first:first + width].astype(F32)
        sig = jax.nn.sigmoid(g)
        g_up = (h * g * sig).astype(BF16)
        g_gate = (h * u * sig * (1.0 + g * (1.0 - sig))).astype(BF16)
        return g_gate, g_up

    def fill(k):
        first, width, at = GROUPS[k]
        g_gate, g_up = grads(first, width)
        gbuf[0, :, at:at + width] = g_gate
        gbuf[0, :, at + width:at + 2 * width] = g_up

    def fill_tail():
        g_gate, g_up = grads(TAIL_FROM, TAIL)
        gbuf[0, :, TAIL_AT:TAIL_AT + LANE] = pack_tail(g_gate, g_up)

    fold_at = CHUNKS[E][0]

    def fold_own():
        for half in range(2):
            rows = slice(half * HALF, (half + 1) * HALF)
            fold[0, :, half * 256:(half + 1) * 256] = gbuf[0, rows, fold_at:fold_at + 256]
        first, second = (
            gbuf[0, half * HALF:(half + 1) * HALF, TAIL_AT:TAIL_AT + LANE].astype(F32)
            for half in range(2)
        )
        fold[0, :, 512:FOLD] = (first + pltpu.roll(second, 32, 1)).astype(BF16)

    def unfold(n):
        lane = lax.broadcasted_iota(jnp.int32, (HALF, LANE), 1)
        kept = lane % 64 < TAIL
        for slot in range(*ROUNDS[n]):
            tails = fold[slot, :, 512:FOLD].astype(F32)
            for half in range(2):
                rows = slice(half * HALF, (half + 1) * HALF)
                gbuf[slot, rows, fold_at:fold_at + 256] = fold[slot, :, half * 256:(half + 1) * 256]
                tail = tails if half == 0 else pltpu.roll(tails, 96, 1)
                gbuf[slot, rows, TAIL_AT:TAIL_AT + LANE] = jnp.where(kept, tail, 0.0).astype(BF16)

    ring = {}
    for k, (start, width) in enumerate(CHUNKS):
        for s in range(1, 5):
            for way in range(2):
                for h in range(2):
                    if s == 4 and way != h:
                        continue
                    sign = -1 if way == 0 else 1
                    src_slot, dst_slot = slot_of(sign * (s - 1)), slot_of(sign * s)
                    rows, columns = pl.ds(h * HALF, HALF), pl.ds(start, width)
                    source, target = (gbuf.at[i, rows, columns] for i in (src_slot, dst_slot))
                    if k == E:
                        rows = pl.ds(h * QR, QR)
                        source, target = fold.at[src_slot, rows], fold.at[dst_slot, rows]
                    ring[k, s, way, h] = remote(
                        source,
                        target,
                        ring_s.at[k, s - 1, way, h], ring_r.at[k, s - 1, way, h],
                        at_z(1 if way == 0 else -1),
                    )

    def step(k, s):
        for turn in range(2):
            for way in range(2):
                h = turn if way == 0 else 1 - turn
                if (k, s, way, h) in ring:
                    if s > 1:
                        ring[k, s - 1, way, h].wait_recv()
                    launch(ring[k, s, way, h])

    def third(k):
        for way in range(2):
            ring[k, 3, way, 1 - way].wait_recv()

    def fourth(k):
        for way in range(2):
            ring[k, 4, way, way].wait_recv()

    q_at = pl.multiple_of(y * QR, 16)
    core_half = pl.ds(pl.multiple_of(c * 256, 256), 256)

    def x_columns(r):
        return pl.ds(pl.multiple_of(((z + r) % NZ) * 512 + c * 256, 256), 256)

    x_first = []
    x_own = pltpu.make_async_copy(
        x_hbm.at[pl.ds(q_at, QR), x_columns(0)],
        xbuf.at[0, pl.ds(q_at, QR), core_half], x1_r.at[0],
    )

    def x_start():
        x_own.start()
        for r in range(1, NZ):
            x_first.append(launch(remote(
                x_hbm.at[pl.ds(q_at, QR), x_columns(r)],
                xbuf.at[slot_of(-r), pl.ds(q_at, QR), core_half],
                x1_s.at[r], x1_r.at[r], at_z(r),
            )))

    def x_second():
        x_own.wait()
        for copy in x_first:
            copy.wait_recv()
        piece = xbuf.at[:, pl.ds(q_at, QR), core_half]
        for e in range(1, NY):
            launch(remote(piece, piece, x2_s.at[e], x2_r.at[e], at_y(e)))

    def x_third():
        for e in range(1, NY):
            rows = pl.ds(pl.multiple_of(((y + NY - e) % NY) * QR, 16), QR)
            there = xbuf.at[:, rows, core_half]
            remote(there, there, x2_s.at[e], x2_r.at[e], at_y(e)).wait_recv()
        mine = xbuf.at[:, :, core_half]
        launch(remote(mine, mine, x3_s, x3_r, sibling))

    def x_turn():
        theirs = xbuf.at[:, :, pl.ds(pl.multiple_of((1 - c) * 256, 256), 256)]
        remote(theirs, theirs, x3_s, x3_r, sibling).wait_recv()
        for j in range(2):
            for i in range(4):
                block = xbuf[2 * i:2 * i + 2, :, j * 256:(j + 1) * 256].reshape(2 * TOK, 256)
                xt[j, :, i * 2 * TOK:(i + 1) * 2 * TOK] = block.T

    mine_w = wt.at[xl]
    w_copy = remote(mine_w, mine_w, w_s, w_r, partner)

    def w_prepare():
        loads[3].wait()
        w_f[:VIEW, :] = w_v[...].astype(F32)
        w_f[VIEW:, :] = jnp.zeros((VIEW_PAD - VIEW, LANE), F32)
        for p in range(2):
            for tile in range(2):
                lanes = slice(tile * LANE, (tile + 1) * LANE)
                for first, width, at in GROUPS + ((TAIL_FROM, 64, TAIL_AT),):
                    piece = w_f[pl.ds(first * 4 + tile * 2 + p, width, stride=4), :]
                    wt[xl, at + p * width:at + (p + 1) * width, lanes] = piece.astype(BF16)
        launch(w_copy)

    def w_wait():
        theirs = wt.at[1 - xl]
        remote(theirs, theirs, w_s, w_r, partner).wait_recv()

    dw_copies = {}

    def dw_product(j, k):
        start, width = CHUNKS[k]
        block = gbuf[:, :, start:start + width].reshape(NZ * TOK, width)
        return jnp.dot(xt[j], block, preferred_element_type=F32)

    def dw_out(k):
        start, width = CHUNKS[k]
        dw_send[:, start:start + width] = dw_product(1 - xl, k).astype(BF16)
        columns = pl.ds(start, width)
        dw_copies[k] = launch(remote(
            dw_send.at[:, columns], dw_recv.at[:, columns], dw_s.at[k], dw_r.at[k], partner
        ))

    def dw_keep(k):
        start, width = CHUNKS[k]
        dw_own[:, start:start + width] = dw_product(xl, k)

    out_copies = []

    def codes_prepare():
        for load in loads[4:]:
            load.wait()
        m_f[:VIEW, :] = mc_v[...].astype(F32)
        s_f[:VIEW, :] = sc_v[...].astype(F32)
        m_f[VIEW:, :] = jnp.zeros((VIEW_PAD - VIEW, LANE), F32)
        s_f[VIEW:, :] = jnp.zeros((VIEW_PAD - VIEW, LANE), F32)

    def column(ref, hidden, p):
        if hidden == TAIL_FROM:
            blank = jnp.ones((1, LANE - TAIL), F32)
            row = jnp.concatenate([ref[p, :, TAIL_FROM:HID], blank], axis=1)
        else:
            row = ref[p, :, hidden:hidden + LANE]
        return jnp.broadcast_to(row, (LANE, LANE)).T

    def top(parts):
        largest = jnp.maximum(jnp.abs(parts[0]), jnp.abs(parts[1]))
        largest = jnp.max(largest, axis=1, keepdims=True) + scale_eps
        return jnp.broadcast_to(largest, parts[0].shape)

    def adam(grads_by_tile, hidden, p):
        count = grads_by_tile[0].shape[0]
        m_scale = beta_first * column(ms_v, hidden, p)[:count]
        s_scale = beta_second * column(ss_v, hidden, p)[:count]
        places = [pl.ds(hidden * 4 + tile * 2 + p, count, stride=4) for tile in range(2)]
        moments, seconds = [], []
        for place, grad in zip(places, grads_by_tile):
            moment = m_f[place, :] * m_scale + (1.0 - beta_first) * grad
            second = s_f[place, :] * s_scale + (1.0 - beta_second) * grad * grad
            scale = jnp.sqrt(second * (1.0 / bias_second)) + adam_eps
            step_v[place, :] = moment * (1.0 / bias_first) / scale
            moments.append(moment)
            seconds.append(second)
        for values, store, new in ((moments, m_f, ms_n), (seconds, s_f, ss_n)):
            largest = top(values)
            if count < LANE:
                new[p, :, TAIL_FROM:HID] = largest.T[:1, :TAIL]
            else:
                new[p, :, hidden:hidden + LANE] = largest.T[:1]
            inverse = 1.0 / largest
            for place, value in zip(places, values):
                store[place, :] = value * inverse

    def dw_end(k):
        dw_copies[k].wait_recv()
        start, width = CHUNKS[k]
        for at in range(start, start + width, LANE):
            columns = slice(at, at + LANE)
            total = (dw_own[:, columns] + dw_recv[:, columns].astype(F32)) * (1.0 / TOKENS)
            total = total.T
            if at == TAIL_AT:
                places = ((0, 64, TAIL_FROM, 0), (64, 64, TAIL_FROM, 1))
            else:
                first, size, begin = [g for g in GROUPS if g[2] <= at][-1]
                p, inner = (at - begin) // size, (at - begin) % size
                places = ((0, LANE, first + inner, p),)
            for lo, count, hidden, p in places:
                adam([total[lo:lo + count, :LANE], total[lo:lo + count, LANE:]], hidden, p)

    def adam_out(i):
        lo, hi = ((0, 1536), (1536, 3072), (3072, VIEW))[i]
        mc_v[lo:hi, :] = m_f[lo:hi, :].astype(BF16)
        sc_v[lo:hi, :] = s_f[lo:hi, :].astype(BF16)
        rows = pl.ds(lo, hi - lo)
        pairs = [(step_v, step_out), (mc_v, mc_out), (sc_v, sc_out)]
        copies = [
            pltpu.make_async_copy(src.at[rows], dst.at[rows], out_sem.at[i, q])
            for q, (src, dst) in enumerate(pairs)
        ]
        if i == 2:
            copies.append(pltpu.make_async_copy(ms_n, ms_out, out_sem.at[i, 3]))
            copies.append(pltpu.make_async_copy(ss_n, ss_out, out_sem.at[i, 4]))
        for copy in copies:
            copy.start()
        out_copies.extend(copies)

    core_copies = {}
    rs_copies = {}

    def dx_away(n):
        lo, hi = ROUNDS[n]
        block = gbuf[lo:hi].reshape((hi - lo) * TOK, PACK)
        there = jnp.dot(block, wt[1 - c], preferred_element_type=F32).astype(BF16)
        c_send[lo:hi] = there.reshape(hi - lo, TOK, 256)
        core_copies[n] = launch(remote(
            c_send.at[lo:hi], c_recv.at[lo:hi], core_s.at[n], core_r.at[n], sibling
        ))

    def dx_keep(n):
        lo, hi = ROUNDS[n]
        block = gbuf[lo:hi].reshape((hi - lo) * TOK, PACK)
        keep[lo:hi] = jnp.dot(block, wt[c], preferred_element_type=F32).reshape(hi - lo, TOK, 256)

    def dx_scatter(n):
        lo, hi = ROUNDS[n]
        core_copies[n].wait_recv()
        rs_src[lo:hi] = (keep[lo:hi] + c_recv[lo:hi].astype(F32)).astype(BF16)
        for e in range(1, NY):
            to = pl.ds(pl.multiple_of(((y + e) % NY) * QR, 16), QR)
            rs_copies[n, e] = launch(remote(
                rs_src.at[lo:hi, to], rs_recv.at[e, lo:hi], rs_s.at[n, e], rs_r.at[n, e], at_y(e)
            ))

    def dx_finish(n):
        lo, hi = ROUNDS[n]
        for e in range(1, NY):
            rs_copies[n, e].wait_recv()
        total = rs_src[lo:hi, pl.ds(q_at, QR)].astype(F32)
        for e in range(1, NY):
            total = total + rs_recv[e, lo:hi].astype(F32)
        if lo == 0:
            f_here[0:1] = total.astype(BF16)
            return
        f_src[lo:hi] = total.astype(BF16)
        for p in range(lo, hi):
            q = slot_of(-REL_OF[p])
            launch(remote(f_src.at[p], f_here.at[q], fz_s.at[q], fz_r.at[q], at_z(REL_OF[p])))

    home_copies = []

    def dx_home(n):
        for p in range(*ROUNDS[n]):
            rel = REL_OF[p]
            if p:
                there = f_here.at[p]
                remote(there, there, fz_s.at[p], fz_r.at[p], at_z(1)).wait_recv()
            chip = (z + rel) % NM
            target = f_buf.at[xh, pl.ds(q_at, QR)]
            away = remote(f_here.at[p], target, fin_s.at[p], fin_r, at_m(chip))
            local = pltpu.make_async_copy(f_here.at[p], target, fin_r)
            here = chip == m
            pl.when(here)(local.start)
            pl.when(jnp.logical_not(here))(away.start)
            home_copies.append((here, away))

    for load in loads[:3]:
        load.wait()
    fill(0)
    pl.semaphore_wait(barrier, len(near))

    step(A, 1)
    tell(z_near, [at_z(1), at_z(-1)])
    tell(y_near, [at_y(1), at_y(-1)])
    step(B, 1)
    for load in loads[3:]:
        load.start()
    fill(1)
    fill(2)
    fill_tail()
    fold_own()
    pl.semaphore_wait(z_near, 2)
    tell(z_far, [at_z(2), at_z(-2)])
    pl.semaphore_wait(y_near, 2)
    tell(plane_in, [at_m(m + 4)])
    step(A, 2)
    w_prepare()
    pl.semaphore_wait(z_far, 2)
    x_start()
    step(B, 2)
    codes_prepare()
    step(A, 3)
    step(C, 1)
    x_second()
    step(A, 4)
    step(B, 3)
    step(C, 2)
    step(B, 4)
    step(D, 1)
    x_third()
    step(C, 3)
    x_turn()
    third(A)
    fourth(A)
    dw_out(A)
    dw_keep(A)
    third(B)
    fourth(B)
    dw_out(B)
    step(D, 2)
    dw_keep(B)
    dw_end(A)
    step(C, 4)
    w_wait()
    dx_away(0)
    step(E, 1)
    dx_keep(0)
    step(D, 3)
    third(C)
    fourth(C)
    dw_out(C)
    dw_keep(C)
    dx_scatter(0)
    step(E, 2)
    unfold(1)
    dx_away(1)
    dx_keep(1)
    step(D, 4)
    dx_scatter(1)
    dw_end(B)
    adam_out(0)
    dx_finish(0)
    step(E, 3)
    pl.semaphore_wait(plane_in, 1)
    dx_home(0)
    unfold(2)
    dx_away(2)
    dx_keep(2)
    dx_scatter(2)
    dx_finish(1)
    third(D)
    fourth(D)
    dw_out(D)
    step(E, 4)
    dw_keep(D)
    third(E)
    unfold(3)
    dx_away(3)
    dx_keep(3)
    dx_scatter(3)
    fourth(E)
    unfold(4)
    dx_away(4)
    dw_out(E)
    dx_keep(4)
    dx_scatter(4)
    dx_finish(2)
    dw_keep(E)
    dx_home(1)
    dx_finish(3)
    dw_end(C)
    dx_finish(4)
    dx_home(2)
    dw_end(D)
    adam_out(1)
    dx_home(3)
    dx_home(4)
    dw_end(E)
    adam_out(2)

    pltpu.make_async_copy(f_buf, f_buf, fin_r).wait()
    out_v[...] = (f_buf[0].astype(F32) + f_buf[1].astype(F32)).astype(BF16)
    result = pltpu.make_async_copy(out_v, ig_out, out_sem.at[0, 3])
    result.start()
    for copy in sends:
        copy.wait_send()
    for here, away in home_copies:
        pl.when(jnp.logical_not(here))(away.wait_send)
    for copy in out_copies:
        copy.wait()
    result.wait()


def compute(*operands):
    hbm = pl.BlockSpec(memory_space=pltpu.HBM)
    dma = pltpu.SemaphoreType.DMA
    regular = pltpu.SemaphoreType.REGULAR
    n = len(CHUNKS)
    return pl.pallas_call(
        comm_kernel,
        out_shape=OUTS,
        in_specs=[hbm] * 9,
        out_specs=[pl.BlockSpec(memory_space=pl.ANY)] * 6,
        scratch_shapes=[
            pltpu.VMEM((TOK, HID), BF16),
            pltpu.VMEM((TOK, HID), BF16),
            pltpu.VMEM((TOK, HID), BF16),
            pltpu.VMEM((VIEW, LANE), BF16),
            pltpu.VMEM((VIEW_PAD, LANE), F32),
            pltpu.VMEM((VIEW, LANE), BF16),
            pltpu.VMEM((VIEW, LANE), BF16),
            pltpu.VMEM((2, 1, HID), F32),
            pltpu.VMEM((2, 1, HID), F32),
            pltpu.VMEM((2, 1, HID), F32),
            pltpu.VMEM((2, 1, HID), F32),
            pltpu.VMEM((VIEW_PAD, LANE), F32),
            pltpu.VMEM((VIEW_PAD, LANE), F32),
            pltpu.VMEM((VIEW_PAD, LANE), F32),
            pltpu.VMEM((NZ, TOK, PACK), BF16),
            pltpu.VMEM((NZ, HALF, FOLD), BF16),
            pltpu.VMEM((NZ, TOK, 512), BF16),
            pltpu.VMEM((2, 256, NZ * TOK), BF16),
            pltpu.VMEM((2, PACK, 256), BF16),
            pltpu.VMEM((ROWS, PACK), BF16),
            pltpu.VMEM((ROWS, PACK), BF16),
            pltpu.VMEM((ROWS, PACK), F32),
            pltpu.VMEM((NZ, TOK, 256), BF16),
            pltpu.VMEM((NZ, TOK, 256), BF16),
            pltpu.VMEM((NZ, TOK, 256), F32),
            pltpu.VMEM((NZ, TOK, 256), BF16),
            pltpu.VMEM((NY, NZ, QR, 256), BF16),
            pltpu.VMEM((NZ, QR, 256), BF16),
            pltpu.VMEM((NZ, QR, 256), BF16),
            pltpu.VMEM((2, TOK, 256), BF16),
            pltpu.VMEM((TOK, 256), BF16),
            dma((8,)),
            dma((n, 4, 2, 2)), dma((n, 4, 2, 2)),
            dma((NZ,)), dma((NZ,)),
            dma((NY,)), dma((NY,)),
            dma, dma, dma, dma,
            dma((n,)), dma((n,)),
            dma((5,)), dma((5,)),
            dma((5, NY)), dma((5, NY)),
            dma((NZ,)), dma((NZ,)),
            dma((NZ,)), dma,
            dma((3, 5)),
            regular, regular, regular, regular,
        ],
        compiler_params=pltpu.CompilerParams(
            collective_id=0, has_side_effects=True, vmem_limit_bytes=60 * 1024 * 1024
        ),
        cost_estimate=pl.CostEstimate(
            flops=6_000_000_000, bytes_accessed=12_000_000, transcendentals=700_000
        ),
    )(*operands)


PIECES = tuple(
    (which, lo, min(lo + 1232, VIEW)) for lo in range(0, VIEW, 1232) for which in (1, 2, 3)
) + ((0, 0, TOK), (4, 0, 2), (5, 0, 2))


def place_kernel(*refs):
    sources, results, held, sem = refs[:6], refs[6:12], refs[12:18], refs[18]

    def moves(n, first, second):
        which, lo, hi = PIECES[n]
        rows = pl.ds(lo, hi - lo)
        return pltpu.make_async_copy(first[which].at[rows], second[which].at[rows], sem.at[n])

    arrivals = [moves(n, sources, held) for n in range(len(PIECES))]
    for copy in arrivals:
        copy.start()
    departures = []
    for n, copy in enumerate(arrivals):
        copy.wait()
        departures.append(moves(n, held, results))
        departures[-1].start()
    for copy in departures:
        copy.wait()


def place(*results):
    hbm = pl.BlockSpec(memory_space=pltpu.HBM)
    return pl.pallas_call(
        place_kernel,
        out_shape=OUTS,
        in_specs=[hbm] * 6,
        out_specs=[hbm] * 6,
        scratch_shapes=[pltpu.VMEM(out.shape, out.dtype) for out in OUTS]
        + [pltpu.SemaphoreType.DMA((len(PIECES),))],
        compiler_params=pltpu.CompilerParams(vmem_limit_bytes=60 * 1024 * 1024),
    )(*results)


def view(a):
    a = a.transpose(2, 0, 1).reshape(HID, 2, 2, LANE)
    return a.transpose(0, 2, 1, 3).reshape(VIEW, LANE)


def unview(a):
    a = a.reshape(HID, 2, 2, LANE).transpose(0, 2, 1, 3)
    return a.reshape(HID, 2, ROWS).transpose(1, 2, 0)


def per_device(x, gate, up, gh, w, mc, sc, ms, ss):
    results = compute(x, gate, up, gh, view(w), view(mc), view(sc), ms, ss)
    ig, step, mc_new, sc_new, ms_new, ss_new = place(*results)
    return ig, unview(step), unview(mc_new), unview(sc_new), ms_new, ss_new


def solution(mesh):
    whole = P(None, "dp", "tensor")
    token = P("dp", "tensor")
    return jax.shard_map(
        per_device,
        mesh=mesh,
        in_specs=(P("dp", None), token, token, token, whole, whole, whole, whole, whole),
        out_specs=(token, whole, whole, whole, whole, whole),
        check_vma=False,
    )
```

```python
import functools

import jax
import jax.numpy as jnp
from jax import lax
from jax.experimental import pallas as pl
from jax.experimental.pallas import tpu as pltpu
from jax.sharding import PartitionSpec as P

MESH = pl.DeviceIdType.MESH
F32 = jnp.float32
BF16 = jnp.bfloat16

beta_first = 0.9
beta_second = 0.95
bias_first = 0.19
bias_second = 0.0975
adam_eps = 1e-08
scale_eps = 1e-06

TOK = 192
HALF = 96
ROWS = 256
HID = 924
PACK = 1920
NZ = 8
NM = 8
NY = 4
TOKENS = 3072
QR = 48
LANE = 128

GROUPS = ((0, 384, 0), (384, 384, 768), (768, 128, 1536))
TAIL_AT = 1792
TAIL_FROM = 896
TAIL = HID - TAIL_FROM
FOLD = 640
CHUNKS = tuple((start, 384) for start in range(0, PACK, 384))
A, B, C, D, E = range(5)
VIEW = 4 * HID
VIEW_PAD = 4 * 960


OUTS = (
    jax.ShapeDtypeStruct((TOK, 256), BF16),
    jax.ShapeDtypeStruct((VIEW, LANE), F32),
    jax.ShapeDtypeStruct((VIEW, LANE), BF16),
    jax.ShapeDtypeStruct((VIEW, LANE), BF16),
    jax.ShapeDtypeStruct((2, 1, HID), F32),
    jax.ShapeDtypeStruct((2, 1, HID), F32),
)


def slot_of(rel):
    rel = rel % NZ
    if rel == 0:
        return 0
    if rel == 4:
        return 7
    return 2 * rel if rel < 4 else 2 * (NZ - rel) - 1


REL_OF = {slot_of(rel): rel for rel in range(NZ)}
ROUNDS = ((0, 1), (1, 3), (3, 5), (5, 7), (7, 8))


def pack_tail(first, second):
    rows = first.shape[0]
    blank = jnp.zeros((rows, 64 - TAIL), first.dtype)
    return jnp.concatenate([first, blank, second, blank], axis=1)


def comm_kernel(
    x_hbm, gate_hbm, up_hbm, gh_hbm, w_hbm, mc_hbm, sc_hbm, ms_hbm, ss_hbm,
    ig_out, step_out, mc_out, sc_out, ms_out, ss_out,
    gate_v, up_v, gh_v, w_v, w_f, mc_v, sc_v, ms_v, ss_v, ms_n, ss_n, m_f, s_f, step_v,
    gbuf, fold, xbuf, xt, wt, dw_send, dw_recv, dw_own, c_send, c_recv, keep, before, rs_src, rs_recv, f_src, f_here, f_buf, out_v,
    load_sem, ring_s, ring_r, x1_s, x1_r, x2_s, x2_r, x3_s, x3_r, w_s, w_r,
    dw_s, dw_r, core_s, core_r, rs_s, rs_r, fz_s, fz_r, fin_s, fin_r, out_sem,
    z_near, z_far, y_near, plane_in,
):
    d = lax.axis_index("dp")
    t = lax.axis_index("tensor")
    z, xl = d // 2, d % 2
    m, c = t // 2, t % 2
    y, xh = m % 4, m // 4

    def at_z(r):
        return (((z + r + NZ) % NZ) * 2 + xl, t)

    def at_y(e):
        return (d, (xh * 4 + (y + e + NY) % NY) * 2 + c)

    def at_m(chip):
        return (d, (chip % NM) * 2 + c)

    sibling = (d, m * 2 + (1 - c))
    partner = (z * 2 + (1 - xl), t)

    loads = [
        pltpu.make_async_copy(gate_hbm, gate_v, load_sem.at[0]),
        pltpu.make_async_copy(up_hbm, up_v, load_sem.at[1]),
        pltpu.make_async_copy(gh_hbm, gh_v, load_sem.at[2]),
        pltpu.make_async_copy(w_hbm, w_v, load_sem.at[3]),
        pltpu.make_async_copy(mc_hbm, mc_v, load_sem.at[4]),
        pltpu.make_async_copy(sc_hbm, sc_v, load_sem.at[5]),
        pltpu.make_async_copy(ms_hbm, ms_v, load_sem.at[6]),
        pltpu.make_async_copy(ss_hbm, ss_v, load_sem.at[7]),
    ]
    for load in loads[:3]:
        load.start()

    def tell(sem, devices):
        for device in devices:
            pl.semaphore_signal(sem, inc=1, device_id=device, device_id_type=MESH)

    barrier = pltpu.get_barrier_semaphore()
    near = [at_z(1), at_z(-1), at_y(1), at_y(-1), at_m(m + 4), sibling, partner]
    tell(barrier, near)

    sends = []

    def remote(src, dst, send_sem, recv_sem, where):
        return pltpu.make_async_remote_copy(
            src_ref=src, dst_ref=dst, send_sem=send_sem, recv_sem=recv_sem,
            device_id=where, device_id_type=MESH,
        )

    def launch(copy):
        copy.start()
        sends.append(copy)
        return copy

    def grads(first, width):
        g = gate_v[:, first:first + width].astype(F32)
        u = up_v[:, first:first + width].astype(F32)
        h = gh_v[:, first:first + width].astype(F32)
        sig = jax.nn.sigmoid(g)
        g_up = (h * g * sig).astype(BF16)
        g_gate = (h * u * sig * (1.0 + g * (1.0 - sig))).astype(BF16)
        return g_gate, g_up

    def fill(k):
        first, width, at = GROUPS[k]
        g_gate, g_up = grads(first, width)
        gbuf[0, :, at:at + width] = g_gate
        gbuf[0, :, at + width:at + 2 * width] = g_up

    def fill_tail():
        g_gate, g_up = grads(TAIL_FROM, TAIL)
        gbuf[0, :, TAIL_AT:TAIL_AT + LANE] = pack_tail(g_gate, g_up)

    fold_at = CHUNKS[E][0]

    def fold_own():
        for half in range(2):
            rows = slice(half * HALF, (half + 1) * HALF)
            fold[0, :, half * 256:(half + 1) * 256] = gbuf[0, rows, fold_at:fold_at + 256]
        first, second = (
            gbuf[0, half * HALF:(half + 1) * HALF, TAIL_AT:TAIL_AT + LANE].astype(F32)
            for half in range(2)
        )
        fold[0, :, 512:FOLD] = (first + pltpu.roll(second, 32, 1)).astype(BF16)

    def unfold(n):
        lane = lax.broadcasted_iota(jnp.int32, (HALF, LANE), 1)
        kept = lane % 64 < TAIL
        for slot in range(*ROUNDS[n]):
            tails = fold[slot, :, 512:FOLD].astype(F32)
            for half in range(2):
                rows = slice(half * HALF, (half + 1) * HALF)
                gbuf[slot, rows, fold_at:fold_at + 256] = fold[slot, :, half * 256:(half + 1) * 256]
                tail = tails if half == 0 else pltpu.roll(tails, 96, 1)
                gbuf[slot, rows, TAIL_AT:TAIL_AT + LANE] = jnp.where(kept, tail, 0.0).astype(BF16)

    ring = {}
    for k, (start, width) in enumerate(CHUNKS):
        for s in range(1, 5):
            for way in range(2):
                for h in range(2):
                    if s == 4 and way != h:
                        continue
                    sign = -1 if way == 0 else 1
                    src_slot, dst_slot = slot_of(sign * (s - 1)), slot_of(sign * s)
                    rows, columns = pl.ds(h * HALF, HALF), pl.ds(start, width)
                    source, target = (gbuf.at[i, rows, columns] for i in (src_slot, dst_slot))
                    if k == E:
                        rows = pl.ds(h * QR, QR)
                        source, target = fold.at[src_slot, rows], fold.at[dst_slot, rows]
                    ring[k, s, way, h] = remote(
                        source,
                        target,
                        ring_s.at[k, s - 1, way, h], ring_r.at[k, s - 1, way, h],
                        at_z(1 if way == 0 else -1),
                    )

    def step(k, s):
        for turn in range(2):
            for way in range(2):
                h = turn if way == 0 else 1 - turn
                if (k, s, way, h) in ring:
                    if s > 1:
                        ring[k, s - 1, way, h].wait_recv()
                    launch(ring[k, s, way, h])

    def third(k):
        for way in range(2):
            ring[k, 3, way, 1 - way].wait_recv()

    def fourth(k):
        for way in range(2):
            ring[k, 4, way, way].wait_recv()

    q_at = pl.multiple_of(y * QR, 16)
    core_half = pl.ds(pl.multiple_of(c * 256, 256), 256)

    def x_columns(r):
        return pl.ds(pl.multiple_of(((z + r) % NZ) * 512 + c * 256, 256), 256)

    x_first = []
    x_own = pltpu.make_async_copy(
        x_hbm.at[pl.ds(q_at, QR), x_columns(0)],
        xbuf.at[0, pl.ds(q_at, QR), core_half], x1_r.at[0],
    )

    def x_start():
        x_own.start()
        for r in range(1, NZ):
            x_first.append(launch(remote(
                x_hbm.at[pl.ds(q_at, QR), x_columns(r)],
                xbuf.at[slot_of(-r), pl.ds(q_at, QR), core_half],
                x1_s.at[r], x1_r.at[r], at_z(r),
            )))

    def x_second():
        x_own.wait()
        for copy in x_first:
            copy.wait_recv()
        piece = xbuf.at[:, pl.ds(q_at, QR), core_half]
        for e in range(1, NY):
            launch(remote(piece, piece, x2_s.at[e], x2_r.at[e], at_y(e)))

    def x_third():
        for e in range(1, NY):
            rows = pl.ds(pl.multiple_of(((y + NY - e) % NY) * QR, 16), QR)
            there = xbuf.at[:, rows, core_half]
            remote(there, there, x2_s.at[e], x2_r.at[e], at_y(e)).wait_recv()
        mine = xbuf.at[:, :, core_half]
        launch(remote(mine, mine, x3_s, x3_r, sibling))

    def x_turn():
        theirs = xbuf.at[:, :, pl.ds(pl.multiple_of((1 - c) * 256, 256), 256)]
        remote(theirs, theirs, x3_s, x3_r, sibling).wait_recv()
        for j in range(2):
            for i in range(4):
                block = xbuf[2 * i:2 * i + 2, :, j * 256:(j + 1) * 256].reshape(2 * TOK, 256)
                xt[j, :, i * 2 * TOK:(i + 1) * 2 * TOK] = block.T

    mine_w = wt.at[xl]
    w_copy = remote(mine_w, mine_w, w_s, w_r, partner)

    def w_prepare():
        loads[3].wait()
        w_f[:VIEW, :] = w_v[...].astype(F32)
        w_f[VIEW:, :] = jnp.zeros((VIEW_PAD - VIEW, LANE), F32)
        for p in range(2):
            for tile in range(2):
                lanes = slice(tile * LANE, (tile + 1) * LANE)
                for first, width, at in GROUPS + ((TAIL_FROM, 64, TAIL_AT),):
                    piece = w_f[pl.ds(first * 4 + tile * 2 + p, width, stride=4), :]
                    wt[xl, at + p * width:at + (p + 1) * width, lanes] = piece.astype(BF16)
        launch(w_copy)

    def w_wait():
        theirs = wt.at[1 - xl]
        remote(theirs, theirs, w_s, w_r, partner).wait_recv()

    dw_copies = {}

    def dw_product(j, k):
        start, width = CHUNKS[k]
        block = gbuf[:, :, start:start + width].reshape(NZ * TOK, width)
        return jnp.dot(xt[j], block, preferred_element_type=F32)

    def dw_out(k):
        start, width = CHUNKS[k]
        dw_send[:, start:start + width] = dw_product(1 - xl, k).astype(BF16)
        columns = pl.ds(start, width)
        dw_copies[k] = launch(remote(
            dw_send.at[:, columns], dw_recv.at[:, columns], dw_s.at[k], dw_r.at[k], partner
        ))

    def dw_keep(k):
        start, width = CHUNKS[k]
        dw_own[:, start:start + width] = dw_product(xl, k)

    out_copies = []

    def codes_prepare():
        for load in loads[4:]:
            load.wait()
        m_f[:VIEW, :] = mc_v[...].astype(F32)
        s_f[:VIEW, :] = sc_v[...].astype(F32)
        m_f[VIEW:, :] = jnp.zeros((VIEW_PAD - VIEW, LANE), F32)
        s_f[VIEW:, :] = jnp.zeros((VIEW_PAD - VIEW, LANE), F32)

    def column(ref, hidden, p):
        if hidden == TAIL_FROM:
            blank = jnp.ones((1, LANE - TAIL), F32)
            row = jnp.concatenate([ref[p, :, TAIL_FROM:HID], blank], axis=1)
        else:
            row = ref[p, :, hidden:hidden + LANE]
        return jnp.broadcast_to(row, (LANE, LANE)).T

    def top(parts):
        largest = jnp.maximum(jnp.abs(parts[0]), jnp.abs(parts[1]))
        largest = jnp.max(largest, axis=1, keepdims=True) + scale_eps
        return jnp.broadcast_to(largest, parts[0].shape)

    def adam(grads_by_tile, hidden, p):
        count = grads_by_tile[0].shape[0]
        m_scale = beta_first * column(ms_v, hidden, p)[:count]
        s_scale = beta_second * column(ss_v, hidden, p)[:count]
        places = [pl.ds(hidden * 4 + tile * 2 + p, count, stride=4) for tile in range(2)]
        moments, seconds = [], []
        for place, grad in zip(places, grads_by_tile):
            moment = m_f[place, :] * m_scale + (1.0 - beta_first) * grad
            second = s_f[place, :] * s_scale + (1.0 - beta_second) * grad * grad
            scale = jnp.sqrt(second * (1.0 / bias_second)) + adam_eps
            step_v[place, :] = moment * (1.0 / bias_first) / scale
            moments.append(moment)
            seconds.append(second)
        for values, store, new in ((moments, m_f, ms_n), (seconds, s_f, ss_n)):
            largest = top(values)
            if count < LANE:
                new[p, :, TAIL_FROM:HID] = largest.T[:1, :TAIL]
            else:
                new[p, :, hidden:hidden + LANE] = largest.T[:1]
            inverse = 1.0 / largest
            for place, value in zip(places, values):
                store[place, :] = value * inverse

    def dw_end(k):
        dw_copies[k].wait_recv()
        start, width = CHUNKS[k]
        for at in range(start, start + width, LANE):
            columns = slice(at, at + LANE)
            total = (dw_own[:, columns] + dw_recv[:, columns].astype(F32)) * (1.0 / TOKENS)
            total = total.T
            if at == TAIL_AT:
                places = ((0, 64, TAIL_FROM, 0), (64, 64, TAIL_FROM, 1))
            else:
                first, size, begin = [g for g in GROUPS if g[2] <= at][-1]
                p, inner = (at - begin) // size, (at - begin) % size
                places = ((0, LANE, first + inner, p),)
            for lo, count, hidden, p in places:
                adam([total[lo:lo + count, :LANE], total[lo:lo + count, LANE:]], hidden, p)

    def adam_out(i):
        lo, hi = ((0, 1536), (1536, 3072), (3072, VIEW))[i]
        mc_v[lo:hi, :] = m_f[lo:hi, :].astype(BF16)
        sc_v[lo:hi, :] = s_f[lo:hi, :].astype(BF16)
        rows = pl.ds(lo, hi - lo)
        pairs = [(step_v, step_out), (mc_v, mc_out), (sc_v, sc_out)]
        copies = [
            pltpu.make_async_copy(src.at[rows], dst.at[rows], out_sem.at[i, q])
            for q, (src, dst) in enumerate(pairs)
        ]
        if i == 2:
            copies.append(pltpu.make_async_copy(ms_n, ms_out, out_sem.at[i, 3]))
            copies.append(pltpu.make_async_copy(ss_n, ss_out, out_sem.at[i, 4]))
        for copy in copies:
            copy.start()
        out_copies.extend(copies)

    core_copies = {}
    rs_copies = {}

    def dx_before():
        block = gbuf[NZ - 1, :, :fold_at]
        for which, j in ((0, 1 - c), (1, c)):
            before[which] = jnp.dot(block, wt[j, :fold_at, :], preferred_element_type=F32)

    def dx_after(which, j):
        block = gbuf[NZ - 1, :, fold_at:]
        product = jnp.dot(block, wt[j, fold_at:, :], preferred_element_type=F32)
        return before[which] + product

    def dx_away(n):
        lo, hi = ROUNDS[n]
        if n == 4:
            there = dx_after(0, 1 - c).astype(BF16)
        else:
            block = gbuf[lo:hi].reshape((hi - lo) * TOK, PACK)
            there = jnp.dot(block, wt[1 - c], preferred_element_type=F32).astype(BF16)
        c_send[lo:hi] = there.reshape(hi - lo, TOK, 256)
        core_copies[n] = launch(remote(
            c_send.at[lo:hi], c_recv.at[lo:hi], core_s.at[n], core_r.at[n], sibling
        ))

    def dx_keep(n):
        lo, hi = ROUNDS[n]
        if n == 4:
            keep[lo:hi] = dx_after(1, c).reshape(1, TOK, 256)
            return
        block = gbuf[lo:hi].reshape((hi - lo) * TOK, PACK)
        keep[lo:hi] = jnp.dot(block, wt[c], preferred_element_type=F32).reshape(hi - lo, TOK, 256)

    def dx_scatter(n):
        lo, hi = ROUNDS[n]
        core_copies[n].wait_recv()
        rs_src[lo:hi] = (keep[lo:hi] + c_recv[lo:hi].astype(F32)).astype(BF16)
        for e in range(1, NY):
            to = pl.ds(pl.multiple_of(((y + e) % NY) * QR, 16), QR)
            rs_copies[n, e] = launch(remote(
                rs_src.at[lo:hi, to], rs_recv.at[e, lo:hi], rs_s.at[n, e], rs_r.at[n, e], at_y(e)
            ))

    def dx_finish(n):
        lo, hi = ROUNDS[n]
        for e in range(1, NY):
            rs_copies[n, e].wait_recv()
        total = rs_src[lo:hi, pl.ds(q_at, QR)].astype(F32)
        for e in range(1, NY):
            total = total + rs_recv[e, lo:hi].astype(F32)
        if lo == 0:
            f_here[0:1] = total.astype(BF16)
            return
        f_src[lo:hi] = total.astype(BF16)
        for p in range(lo, hi):
            q = slot_of(-REL_OF[p])
            launch(remote(f_src.at[p], f_here.at[q], fz_s.at[q], fz_r.at[q], at_z(REL_OF[p])))

    home_copies = []

    def dx_home(n):
        for p in range(*ROUNDS[n]):
            rel = REL_OF[p]
            if p:
                there = f_here.at[p]
                remote(there, there, fz_s.at[p], fz_r.at[p], at_z(1)).wait_recv()
            chip = (z + rel) % NM
            target = f_buf.at[xh, pl.ds(q_at, QR)]
            away = remote(f_here.at[p], target, fin_s.at[p], fin_r, at_m(chip))
            local = pltpu.make_async_copy(f_here.at[p], target, fin_r)
            here = chip == m
            pl.when(here)(local.start)
            pl.when(jnp.logical_not(here))(away.start)
            home_copies.append((here, away))

    for load in loads[:3]:
        load.wait()
    fill(0)
    pl.semaphore_wait(barrier, len(near))

    step(A, 1)
    tell(z_near, [at_z(1), at_z(-1)])
    tell(y_near, [at_y(1), at_y(-1)])
    step(B, 1)
    for load in loads[3:]:
        load.start()
    fill(1)
    fill(2)
    fill_tail()
    fold_own()
    pl.semaphore_wait(z_near, 2)
    tell(z_far, [at_z(2), at_z(-2)])
    pl.semaphore_wait(y_near, 2)
    tell(plane_in, [at_m(m + 4)])
    step(A, 2)
    w_prepare()
    pl.semaphore_wait(z_far, 2)
    x_start()
    step(B, 2)
    codes_prepare()
    step(A, 3)
    step(C, 1)
    x_second()
    step(A, 4)
    step(B, 3)
    step(C, 2)
    step(B, 4)
    step(D, 1)
    x_third()
    step(C, 3)
    x_turn()
    third(A)
    fourth(A)
    dw_out(A)
    dw_keep(A)
    third(B)
    fourth(B)
    dw_out(B)
    step(D, 2)
    dw_keep(B)
    dw_end(A)
    step(C, 4)
    w_wait()
    dx_away(0)
    step(E, 1)
    dx_keep(0)
    step(D, 3)
    third(C)
    fourth(C)
    dw_out(C)
    dw_keep(C)
    dx_scatter(0)
    step(E, 2)
    unfold(1)
    dx_away(1)
    dx_keep(1)
    step(D, 4)
    dx_scatter(1)
    dw_end(B)
    adam_out(0)
    dx_finish(0)
    step(E, 3)
    pl.semaphore_wait(plane_in, 1)
    dx_home(0)
    unfold(2)
    dx_away(2)
    dx_keep(2)
    dx_scatter(2)
    dx_finish(1)
    third(D)
    fourth(D)
    dw_out(D)
    step(E, 4)
    dx_before()
    third(E)
    unfold(3)
    dx_away(3)
    dx_keep(3)
    dx_scatter(3)
    fourth(E)
    unfold(4)
    dx_away(4)
    dw_out(E)
    dx_keep(4)
    dx_scatter(4)
    dw_keep(D)
    dx_finish(2)
    dw_keep(E)
    dx_home(1)
    dx_finish(3)
    dw_end(C)
    dx_finish(4)
    dx_home(2)
    dw_end(D)
    adam_out(1)
    dx_home(3)
    dx_home(4)
    dw_end(E)
    adam_out(2)

    pltpu.make_async_copy(f_buf, f_buf, fin_r).wait()
    out_v[...] = (f_buf[0].astype(F32) + f_buf[1].astype(F32)).astype(BF16)
    result = pltpu.make_async_copy(out_v, ig_out, out_sem.at[0, 3])
    result.start()
    for copy in sends:
        copy.wait_send()
    for here, away in home_copies:
        pl.when(jnp.logical_not(here))(away.wait_send)
    for copy in out_copies:
        copy.wait()
    result.wait()


def compute(*operands):
    hbm = pl.BlockSpec(memory_space=pltpu.HBM)
    dma = pltpu.SemaphoreType.DMA
    regular = pltpu.SemaphoreType.REGULAR
    n = len(CHUNKS)
    return pl.pallas_call(
        comm_kernel,
        out_shape=OUTS,
        in_specs=[hbm] * 9,
        out_specs=[pl.BlockSpec(memory_space=pl.ANY)] * 6,
        scratch_shapes=[
            pltpu.VMEM((TOK, HID), BF16),
            pltpu.VMEM((TOK, HID), BF16),
            pltpu.VMEM((TOK, HID), BF16),
            pltpu.VMEM((VIEW, LANE), BF16),
            pltpu.VMEM((VIEW_PAD, LANE), F32),
            pltpu.VMEM((VIEW, LANE), BF16),
            pltpu.VMEM((VIEW, LANE), BF16),
            pltpu.VMEM((2, 1, HID), F32),
            pltpu.VMEM((2, 1, HID), F32),
            pltpu.VMEM((2, 1, HID), F32),
            pltpu.VMEM((2, 1, HID), F32),
            pltpu.VMEM((VIEW_PAD, LANE), F32),
            pltpu.VMEM((VIEW_PAD, LANE), F32),
            pltpu.VMEM((VIEW_PAD, LANE), F32),
            pltpu.VMEM((NZ, TOK, PACK), BF16),
            pltpu.VMEM((NZ, HALF, FOLD), BF16),
            pltpu.VMEM((NZ, TOK, 512), BF16),
            pltpu.VMEM((2, 256, NZ * TOK), BF16),
            pltpu.VMEM((2, PACK, 256), BF16),
            pltpu.VMEM((ROWS, PACK), BF16),
            pltpu.VMEM((ROWS, PACK), BF16),
            pltpu.VMEM((ROWS, PACK), F32),
            pltpu.VMEM((NZ, TOK, 256), BF16),
            pltpu.VMEM((NZ, TOK, 256), BF16),
            pltpu.VMEM((NZ, TOK, 256), F32),
            pltpu.VMEM((2, TOK, 256), F32),
            pltpu.VMEM((NZ, TOK, 256), BF16),
            pltpu.VMEM((NY, NZ, QR, 256), BF16),
            pltpu.VMEM((NZ, QR, 256), BF16),
            pltpu.VMEM((NZ, QR, 256), BF16),
            pltpu.VMEM((2, TOK, 256), BF16),
            pltpu.VMEM((TOK, 256), BF16),
            dma((8,)),
            dma((n, 4, 2, 2)), dma((n, 4, 2, 2)),
            dma((NZ,)), dma((NZ,)),
            dma((NY,)), dma((NY,)),
            dma, dma, dma, dma,
            dma((n,)), dma((n,)),
            dma((5,)), dma((5,)),
            dma((5, NY)), dma((5, NY)),
            dma((NZ,)), dma((NZ,)),
            dma((NZ,)), dma,
            dma((3, 5)),
            regular, regular, regular, regular,
        ],
        compiler_params=pltpu.CompilerParams(
            collective_id=0, has_side_effects=True, vmem_limit_bytes=60 * 1024 * 1024
        ),
        cost_estimate=pl.CostEstimate(
            flops=6_000_000_000, bytes_accessed=12_000_000, transcendentals=700_000
        ),
    )(*operands)


PIECES = tuple(
    (which, lo, min(lo + 528, VIEW)) for lo in range(0, VIEW, 528) for which in (1, 2, 3)
) + ((0, 0, TOK), (4, 0, 2), (5, 0, 2))


def place_kernel(*refs):
    sources, results, held, sem = refs[:6], refs[6:12], refs[12:18], refs[18]

    def moves(n, first, second):
        which, lo, hi = PIECES[n]
        rows = pl.ds(lo, hi - lo)
        return pltpu.make_async_copy(first[which].at[rows], second[which].at[rows], sem.at[n])

    arrivals = [moves(n, sources, held) for n in range(len(PIECES))]
    for copy in arrivals:
        copy.start()
    departures = []
    for n, copy in enumerate(arrivals):
        copy.wait()
        departures.append(moves(n, held, results))
        departures[-1].start()
    for copy in departures:
        copy.wait()


def place(*results):
    hbm = pl.BlockSpec(memory_space=pltpu.HBM)
    return pl.pallas_call(
        place_kernel,
        out_shape=OUTS,
        in_specs=[hbm] * 6,
        out_specs=[hbm] * 6,
        scratch_shapes=[pltpu.VMEM(out.shape, out.dtype) for out in OUTS]
        + [pltpu.SemaphoreType.DMA((len(PIECES),))],
        compiler_params=pltpu.CompilerParams(vmem_limit_bytes=60 * 1024 * 1024),
    )(*results)


def view(a):
    a = a.transpose(2, 0, 1).reshape(HID, 2, 2, LANE)
    return a.transpose(0, 2, 1, 3).reshape(VIEW, LANE)


def unview(a):
    a = a.reshape(HID, 2, 2, LANE).transpose(0, 2, 1, 3)
    return a.reshape(HID, 2, ROWS).transpose(1, 2, 0)


def per_device(x, gate, up, gh, w, mc, sc, ms, ss):
    results = compute(x, gate, up, gh, view(w), view(mc), view(sc), ms, ss)
    ig, step, mc_new, sc_new, ms_new, ss_new = place(*results)
    return ig, unview(step), unview(mc_new), unview(sc_new), ms_new, ss_new


def solution(mesh):
    whole = P(None, "dp", "tensor")
    token = P("dp", "tensor")
    return jax.shard_map(
        per_device,
        mesh=mesh,
        in_specs=(P("dp", None), token, token, token, whole, whole, whole, whole, whole),
        out_specs=(token, whole, whole, whole, whole, whole),
        check_vma=False,
    )
```
